512 devices in a mesh: dp: 8 (over y, core), expert: 64 (over x, z).
Axes of the slice: x: 4, y: 4, z: 16, core: 2. Of those that a mesh axis runs over, the one named last changes fastest.
Arguments:
- master: float32 [64, 1024, 1152], P('expert', 'dp'), may hold values from -1 to 1
- moment_one: float32 [64, 1024, 1152], P('expert', 'dp'), may hold values from -6 to 6
- moment_two: float32 [64, 1024, 1152], P('expert', 'dp'), may hold values from 0.25 to 4
- gradients: bfloat16 [64, 1024, 1152], P('expert', 'dp'), may hold values from -40 to 40
- old_host: int32 [64], replicated, may hold values from 0 to 63, as said below
- new_host: int32 [64], replicated, may hold values from 0 to 63, as said below
- tokens: bfloat16 [65536, 1024], P(('dp', 'expert')), may hold values from -6 to 6
- routes: int32 [65536, 8], P(('dp', 'expert')), may hold values from 0 to 63, all different within a row; in each aligned block of 128 rows (0 to 127, 128 to 255, ...) at most 24 rows name the same one
- route_weights: float32 [65536, 8], P(('dp', 'expert')), may hold values from 0.02 to 0.5
Outputs:
- new_master: float32 [64, 1024, 1152], P('expert', 'dp')
- new_moment_one: float32 [64, 1024, 1152], P('expert', 'dp')
- new_moment_two: float32 [64, 1024, 1152], P('expert', 'dp')
- mixed: bfloat16 [65536, 1024], P(('dp', 'expert'))
The draws below stay inside these ranges and needn't reach their ends.
Inputs may be any that keep to these rules, and one draw needn't show every extreme that they name: old_host places the 64 experts on distinct hosts. new_host places the 64 experts on distinct hosts; exactly 16 experts have a new_host different from their old_host. `routes`: each token names 8 different experts; among the 128 tokens of one device no expert is named by more than 24 tokens, and in every draw some device has an expert named by exactly 24 of its tokens.
All inputs are finite; a program needn't handle non-finite values.
Results may differ from the reference program's by a relative error of at most 0.0076.
Values may be sent and summed in bfloat16 or wider, within the bound.
No kernel may reach another device: no remote copies, remote signals or barrier semaphores. Data moves between devices by JAX's collectives and lax.ppermute only.
A program may use at most 64 MiB of HBM per device.

```python
import math
import jax
import jax.numpy as jnp
import numpy as np
from jax import lax

D = 1024
F = 384
TOP = 8
MOVED = 16
TOK_DEV = 128
EXPERTS = 64
CAP = 24
TOKENS = 65536
N_DP = 8
N_EXPERT = 64


def plan_pair(key):
    first = jax.random.permutation(jax.random.fold_in(key, 11), EXPERTS).astype(jnp.int32)
    shuffle = jax.random.permutation(jax.random.fold_in(key, 12), EXPERTS).astype(jnp.int32)
    position_ids = jnp.arange(EXPERTS, dtype=jnp.int32)
    partner = jnp.where(position_ids < MOVED, shuffle[(position_ids + 1) % MOVED], shuffle)
    second = first.at[shuffle].set(first[partner])
    return (first, second)


def draw_old_host(key, part):
    return plan_pair(key)[0]


def draw_new_host(key, part):
    return plan_pair(key)[1]


def draw_master(key, part):
    key = jax.random.fold_in(key, 3)
    column = jnp.arange(3 * F)
    column_scale = jnp.where(column < 2 * F, D ** (-0.5), F ** (-0.5)).astype(jnp.float32)
    sample = jnp.clip(jax.random.normal(key, (EXPERTS, D, 3 * F), jnp.float32), -4.0, 4.0)
    return sample * column_scale[None, None, :]


def draw_gradients(key, part):
    key = jax.random.fold_in(key, 5)
    rising = 1.0 + 2.0 * jnp.arange(EXPERTS, dtype=jnp.float32) / max(EXPERTS - 1, 1)
    sample = jnp.clip(jax.random.normal(key, (EXPERTS, D, 3 * F), jnp.float32), -4.0, 4.0)
    return (sample * rising[:, None, None]).astype(jnp.bfloat16)


def shard_levels(own_key, extent, cuts, least, high):
    def one(dim, shards_of):
        heights = jax.random.uniform(jax.random.fold_in(jax.random.fold_in(own_key, 6), dim), (shards_of,), jnp.float32, least / len(cuts), high / len(cuts))
        return jnp.repeat(jnp.exp(heights), extent[dim] // shards_of).reshape((-1,) + (1,) * (len(extent) - dim - 1))

    loudness = one(*cuts[0])
    for cut in cuts[1:]:
        loudness = loudness * one(*cut)
    return loudness


def routed_block(own_key, own, number, rows, count, top, most, skew):
    sequence = jax.random.permutation(own_key, count)
    packed, ordinary = portions_of(count, rows * top, most, skew, True), portions_of(count, rows * top, most, skew, False)
    places = jnp.arange(count)

    def named(tallies, turn):
        used = int((tallies > 0).sum())
        fixed = max(1, used // 4)
        shifted = fixed + (places - fixed + turn * (used - fixed)) % max(1, count - fixed)
        return jnp.zeros((count,), jnp.int32).at[sequence[jnp.where(places < fixed, places, shifted)]].set(jnp.asarray(tallies, jnp.int32))

    tallies = jnp.where(number % 4 == 0, named(packed, number // 4), named(ordinary, number - number // 4 - 1))
    mixed = jax.random.permutation(jax.random.fold_in(own, 3), count)
    donor, sink = mixed[0:count // 2 * 2:2], mixed[1:count // 2 * 2:2]
    margin = jnp.minimum(tallies[donor] - 1, most - tallies[sink]) // 2
    margin = jnp.where((donor == sequence[0]) | (sink == sequence[0]) | (tallies[sink] == 0), 0, jnp.maximum(margin, 0))
    shifted = jax.random.randint(jax.random.fold_in(own, 4), (count // 2,), 0, 1 << 20) % (margin + 1)
    tallies = tallies.at[donor].add(-shifted).at[sink].add(shifted)
    items = jnp.searchsorted(jnp.cumsum(tallies), jnp.arange(rows * top), side="right").astype(jnp.int32)
    grid = items.reshape(top, rows).T
    grid = grid[jax.random.permutation(jax.random.fold_in(own, 1), rows)]
    turn = jax.random.randint(jax.random.fold_in(own, 2), (rows, 1), 0, top)
    return jnp.take_along_axis(grid, (jnp.arange(top)[None, :] + turn) % top, axis=1)


def portions_of(count, total, bound, skew, full):
    portions = [(1 << 20) // math.isqrt(rank ** skew) + 1 for rank in range(1, count + 1)]
    largest = bound if full else min(bound, max(-(-total // count), total * portions[0] // sum(portions)))
    least = 1 if total - largest >= count - 1 else 0
    counts, spare = [largest] + [least] * (count - 1), total - largest - least * (count - 1)
    while spare > 0:
        free = [i for i in range(1, count) if counts[i] < largest] or [i for i in range(1, count) if counts[i] < bound]
        mass, budget = sum([portions[i] for i in free]), spare
        for i in free:
            more = min(bound - counts[i], max(1, budget * portions[i] // mass), spare)
            counts[i] = counts[i] + more
            spare = spare - more
    return np.array(counts)


def normal_values(stream_key, shape, deviation, bound, pieces=(), held_as=jnp.bfloat16):
    entries = deviation * jax.random.normal(stream_key, shape, jnp.float32)
    if pieces:
        entries = entries * shard_levels(stream_key, shape, pieces, -0.22, 0.18)
    return jnp.clip(entries, -bound, bound).astype(held_as)


def setup_inputs(seed: int = 0) -> dict:
    keys = jax.random.split(jax.random.key(seed), 10)
    master = draw_master(jax.random.fold_in(keys[9], 71), 0)
    moment_one = normal_values(keys[1], (EXPERTS, D, 3 * F), 1.0, 6.0, ((0, 64), (1, 8)), jnp.float32)
    moment_two = jnp.clip(jnp.exp(math.log(4.0) - 2.7725887 * jax.random.uniform(keys[2], (EXPERTS, D, 3 * F), jnp.float32) ** shard_levels(keys[2], (EXPERTS, D, 3 * F), ((0, 64), (1, 8)), -0.2, 0.2)), 0.25, 4.0)
    gradients = draw_gradients(jax.random.fold_in(keys[9], 71), 0)
    old_host = draw_old_host(jax.random.fold_in(keys[9], 71), 0)
    new_host = draw_new_host(jax.random.fold_in(keys[9], 71), 0)
    tokens = normal_values(keys[6], (TOKENS, D), 1.0, 6.0, ((0, 512),))
    routes_keys = jax.random.split(jax.random.fold_in(keys[7], 1), TOKENS // TOK_DEV)
    routes_turns = jax.random.permutation(jax.random.fold_in(keys[7], 3), TOKENS // TOK_DEV)
    routes = jax.vmap(lambda own, number: routed_block(jax.random.fold_in(keys[7], 2), own, number, TOK_DEV, EXPERTS, TOP, CAP, 2))(routes_keys, routes_turns).reshape((TOKENS, TOP))
    route_weights = jnp.clip(jnp.exp(math.log(0.5) - 3.218876 * jax.random.uniform(keys[8], (TOKENS, TOP), jnp.float32) ** shard_levels(keys[8], (TOKENS, TOP), ((0, 512),), -0.2, 0.2)), 0.02, 0.5)
    return dict(master=master, moment_one=moment_one, moment_two=moment_two, gradients=gradients, old_host=old_host, new_host=new_host, tokens=tokens, routes=routes, route_weights=route_weights)


beta_one = 0.9
beta_two = 0.95
epsilon = 1e-08
learn_rate = 0.001
decay_rate = 0.1
step_count = 10

def adamw(master, moment_one, moment_two, gradients, factor):
    scaled = gradients.astype(jnp.float32) * factor
    new_one = beta_one * moment_one + (1.0 - beta_one) * scaled
    new_two = beta_two * moment_two + (1.0 - beta_two) * scaled * scaled
    corrected_one = new_one / (1.0 - beta_one ** step_count)
    corrected_two = new_two / (1.0 - beta_two ** step_count)
    step_size = corrected_one / (jnp.sqrt(corrected_two) + epsilon) + decay_rate * master
    return (master - learn_rate * step_size, new_one, new_two)

def reference(master, moment_one, moment_two, gradients, old_host, new_host, tokens, routes, route_weights):
    square_sum = jnp.sum(jnp.square(gradients.astype(jnp.float32)))
    clip_limit = jnp.sqrt(jnp.asarray(EXPERTS * D * 3 * F, jnp.float32))
    factor = jnp.minimum(1.0, clip_limit / (jnp.sqrt(square_sum) + 1e-06))
    updated_master, updated_one, updated_two = adamw(master, moment_one, moment_two, gradients, factor)
    expert_ids = jnp.arange(EXPERTS, dtype=jnp.int32)
    owner = jnp.zeros((EXPERTS,), jnp.int32).at[new_host].set(expert_ids)
    source = old_host[owner]
    new_master = updated_master[source]
    new_moment_one = updated_one[source]
    new_moment_two = updated_two[source]
    devices = N_DP * N_EXPERT
    per_device = TOK_DEV * TOP

    def slots(dev_routes):
        onehot = (dev_routes[:, None] == expert_ids[None, :]).astype(jnp.int32)
        earlier = lax.optimization_barrier(jnp.sum((jnp.cumsum(onehot, axis=0) - onehot) * onehot, axis=1))
        position = dev_routes * CAP + earlier
        empty = jnp.full((EXPERTS * CAP,), per_device, jnp.int32)
        return empty.at[position].set(jnp.arange(per_device, dtype=jnp.int32))
    slot_table = lax.map(slots, routes.reshape(devices, per_device))
    offsets = (jnp.arange(devices, dtype=jnp.int32) * per_device)[:, None]
    global_ids = jnp.where(slot_table < per_device, slot_table + offsets, TOKENS * TOP)
    global_ids = global_ids.reshape(devices, EXPERTS, CAP).transpose(1, 0, 2).reshape(EXPERTS, devices * CAP)
    padded_tokens = jnp.concatenate([tokens, jnp.zeros((1, D), tokens.dtype)], axis=0)
    padded_weights = jnp.concatenate([route_weights.reshape(-1), jnp.zeros((1,), route_weights.dtype)])

    def one_expert(mixture, inputs):
        expert, assign = inputs
        weights = lax.optimization_barrier(new_master[new_host[expert]].astype(jnp.bfloat16)).astype(jnp.float32)
        row_data = padded_tokens[assign // TOP].astype(jnp.float32)
        projected = jnp.dot(row_data, weights[:, :2 * F], preferred_element_type=jnp.float32)
        hidden = (jax.nn.silu(projected[:, :F]) * projected[:, F:]).astype(jnp.bfloat16)
        hidden = lax.optimization_barrier(hidden).astype(jnp.float32)
        produced = jnp.dot(hidden, weights[:, 2 * F:].T, preferred_element_type=jnp.float32).astype(jnp.bfloat16)
        weight_rows = padded_weights[assign]
        mixture = mixture.at[assign // TOP].add(weight_rows[:, None] * produced.astype(jnp.float32), mode='drop')
        return (mixture, None)
    mixture, unused = lax.scan(one_expert, jnp.zeros((TOKENS, D), jnp.float32), (expert_ids, global_ids))
    return (new_master, new_moment_one, new_moment_two, mixture.astype(jnp.bfloat16))
```

```python
import jax
import jax.numpy as jnp
from jax import lax
from jax.sharding import Mesh, PartitionSpec as P

beta_one = 0.9
beta_two = 0.95
epsilon = 1e-08
learn_rate = 0.001
decay_rate = 0.1
step_count = 10

Y, CORE, X, Z = 4, 2, 4, 16
DP = ("y", "c")
PLANE = ("y", "c", "x")
SHARE = Z // (Y * CORE)
bf16, f32 = jnp.bfloat16, jnp.float32


def adamw(master, moment_one, moment_two, gradients, factor):
    scaled = gradients.astype(f32) * factor
    new_one = beta_one * moment_one + (1.0 - beta_one) * scaled
    new_two = beta_two * moment_two + (1.0 - beta_two) * scaled * scaled
    corrected_one = new_one / (1.0 - beta_one**step_count)
    corrected_two = new_two / (1.0 - beta_two**step_count)
    step_size = corrected_one / (jnp.sqrt(corrected_two) + epsilon) + decay_rate * master
    return (master - learn_rate * step_size, new_one, new_two)


def swap(array, axes):
    return lax.all_to_all(array, axes, split_axis=0, concat_axis=0, tiled=True)


def total(value, axes):
    count = lax.axis_size(axes)
    sent = jnp.broadcast_to(value, (count, 1, 128))
    return jnp.sum(swap(sent, axes)[:, 0, 0])


def per_device(
    master, moment_one, moment_two, gradients, old_host, new_host, tokens, routes, route_weights
):
    master, moment_one, moment_two, gradients = (
        item[0] for item in (master, moment_one, moment_two, gradients)
    )
    rows, cols = master.shape
    host_count = X * Z
    my_x, my_z = lax.axis_index("x"), lax.axis_index("z")
    my_host = my_x * Z + my_z
    hosts = jnp.arange(host_count, dtype=jnp.int32)

    local_sum = jnp.sum(jnp.square(gradients.astype(f32)))
    square_sum = total(total(local_sum, PLANE), "z")
    element_count = host_count * Y * CORE * rows * cols
    factor = jnp.minimum(1.0, jnp.sqrt(f32(element_count)) / (jnp.sqrt(square_sum) + 1e-06))

    owner_hot = (new_host[None, :] == hosts[:, None]).astype(jnp.int32)
    source = jnp.sum(owner_hot * old_host[None, :], axis=1)

    tok_count, width = tokens.shape
    top = routes.shape[1]
    capacity = 3 * tok_count * top // (2 * host_count)
    place = ((old_host % Z) // SHARE * X + old_host // Z) * SHARE + old_host % SHARE
    route_place = jnp.sum(
        jnp.where(routes[:, :, None] == hosts[None, None, :], place[None, None, :], 0), axis=2
    ).T
    hits = route_place[None, :, :] == hosts[:, None, None]
    chosen = jnp.any(hits, axis=1)
    gate = jnp.sum(jnp.where(hits, route_weights.T[None, :, :], 0.0), axis=1)
    token_ids = jnp.arange(tok_count, dtype=jnp.int32)
    before = (token_ids[:, None] < token_ids[None, :]).astype(bf16)
    rank = jnp.dot(chosen.astype(bf16), before, preferred_element_type=f32)
    slot = jnp.where(chosen, rank, -1.0)
    slot_ids = jnp.arange(capacity, dtype=jnp.int32).astype(f32)
    taken = slot[:, None, :] == slot_ids[None, :, None]
    pick = taken.astype(bf16).reshape(-1, tok_count)
    outgoing = jnp.dot(pick, tokens, preferred_element_type=f32).astype(bf16)
    outgoing = outgoing.reshape(Y * CORE * X, SHARE * capacity, width)
    mix = jnp.where(taken, gate[:, None, :], 0.0).reshape(-1, tok_count)
    mix_high = mix.astype(bf16)
    mix_low = (mix - mix_high.astype(f32)).astype(bf16)
    outgoing, factor = lax.optimization_barrier((outgoing, factor))

    new_master, new_one, new_two = adamw(master, moment_one, moment_two, gradients, factor)
    gathered = lax.all_gather(new_master.astype(bf16), "z", axis=0, tiled=True)
    moments = jnp.stack([new_one.astype(bf16), new_two.astype(bf16)])
    quarter = rows // X
    moments = moments.reshape(2, X, quarter, cols).transpose(1, 0, 2, 3)
    received = swap(outgoing, PLANE)
    moments, received = lax.optimization_barrier((moments, received))
    moments = swap(moments, "x")
    moments, gathered, received = lax.optimization_barrier((moments, gathered, received))
    moments = lax.all_gather(moments.reshape(-1, cols), "z", axis=0, tiled=True)

    planes = gathered.reshape(Z, rows, cols)
    weights = swap(gathered.reshape(Y * CORE, SHARE * rows, cols), DP)
    weights = weights.reshape(Y * CORE, SHARE, rows, cols)
    hidden_units = cols // 3
    inputs = received.reshape(-1, SHARE, capacity, width)
    outs = []
    for j in range(SHARE):
        weight = weights[:, j].reshape(-1, cols)
        rows_in = inputs[:, j].reshape(-1, width)
        projected = jnp.dot(rows_in, weight[:, : 2 * hidden_units], preferred_element_type=f32)
        hidden = (jax.nn.silu(projected[:, :hidden_units]) * projected[:, hidden_units:]).astype(bf16)
        produced = lax.dot_general(
            hidden,
            weight[:, 2 * hidden_units :],
            (((1,), (1,)), ((), ())),
            preferred_element_type=f32,
        )
        outs.append(produced.astype(bf16).reshape(-1, capacity, width))
    results = jnp.stack(outs, axis=1).reshape(received.shape)
    returned = swap(results, PLANE).reshape(-1, width)
    contract = (((0,), (0,)), ((), ()))
    mixed = lax.dot_general(mix_high, returned, contract, preferred_element_type=f32)
    mixed += lax.dot_general(mix_low, returned, contract, preferred_element_type=f32)
    mixed = mixed.astype(bf16)

    plane_source = source.reshape(X, Z)[:, my_z]
    src_x, src_z = plane_source // Z, plane_source % Z
    sent = jnp.stack([lax.dynamic_index_in_dim(planes, src_z[i], 0, False) for i in range(X)])
    sent, returned = lax.optimization_barrier((sent, returned))
    arrived = swap(sent, "x")
    moved_master = lax.dynamic_index_in_dim(arrived, src_x[my_x], 0, False)
    pieces = moments.reshape(Z, X, 2, quarter, cols)
    sent = jnp.stack(
        [
            lax.dynamic_slice(pieces, (src_z[i], src_x[i], 0, 0, 0), (1, 1, 2, quarter, cols))[0, 0]
            for i in range(X)
        ]
    )
    arrived = swap(sent, "x")
    moved_moments = arrived.transpose(1, 0, 2, 3).reshape(2, rows, cols)
    moved = source[my_host] != my_host
    return (
        jnp.where(moved, moved_master.astype(f32), new_master)[None],
        jnp.where(moved, moved_moments[0].astype(f32), new_one)[None],
        jnp.where(moved, moved_moments[1].astype(f32), new_two)[None],
        mixed,
    )


def solution(mesh):
    fine = Mesh(mesh.devices.reshape(Y, CORE, X, Z), ("y", "c", "x", "z"))
    state = P(("x", "z"), DP, None)
    rows = P(("y", "c", "x", "z"), None)
    return jax.shard_map(
        per_device,
        mesh=fine,
        in_specs=(state, state, state, state, P(), P(), rows, rows, rows),
        out_specs=(state, state, state, rows),
        check_vma=False,
    )
```

```python
import jax
import jax.numpy as jnp
from jax import lax
from jax.experimental import pallas as pl
from jax.sharding import Mesh, PartitionSpec as P

beta_one = 0.9
beta_two = 0.95
epsilon = 1e-08
learn_rate = 0.001
decay_rate = 0.1
step_count = 10

Y, CORE, X, Z = 4, 2, 4, 16
DP = ("y", "c")
PLANE = ("y", "c", "x")
SHARE = Z // (Y * CORE)
bf16, f32 = jnp.bfloat16, jnp.float32


def adamw(master, moment_one, moment_two, gradients, factor):
    scaled = gradients.astype(f32) * factor
    new_one = beta_one * moment_one + (1.0 - beta_one) * scaled
    new_two = beta_two * moment_two + (1.0 - beta_two) * scaled * scaled
    corrected_one = new_one / (1.0 - beta_one**step_count)
    corrected_two = new_two / (1.0 - beta_two**step_count)
    step_size = corrected_one / (jnp.sqrt(corrected_two) + epsilon) + decay_rate * master
    return (master - learn_rate * step_size, new_one, new_two)


def swap(array, axes):
    return lax.all_to_all(array, axes, split_axis=0, concat_axis=0, tiled=True)


def spread_squares(values, sent):
    value = values[...].astype(f32)
    sent[...] = jnp.full(sent.shape, jnp.sum(value * value), f32)


def spread_sum(values, sent):
    sent[...] = jnp.broadcast_to(jnp.sum(values[...], axis=0, keepdims=True), sent.shape)


def spread(kernel, operand, axes):
    return pl.pallas_call(
        kernel, out_shape=jax.ShapeDtypeStruct((lax.axis_size(axes), 1, 128), f32)
    )(operand)


def shifted(blocks, size):
    return [
        lax.ppermute(block, "x", [(i, (i + shift) % size) for i in range(size)])
        for shift, block in enumerate(blocks, 1)
    ]


def per_device(
    master, moment_one, moment_two, gradients, old_host, new_host, tokens, routes, route_weights
):
    master, moment_one, moment_two, gradients = (
        item[0] for item in (master, moment_one, moment_two, gradients)
    )
    rows, cols = master.shape
    host_count = X * Z
    my_x, my_z = lax.axis_index("x"), lax.axis_index("z")
    my_host = my_x * Z + my_z
    hosts = jnp.arange(host_count, dtype=jnp.int32)

    squares = swap(spread(spread_squares, gradients, PLANE), PLANE)
    squares = swap(spread(spread_sum, squares, "z"), "z")
    square_sum = jnp.sum(squares[:, 0, 0])
    element_count = host_count * Y * CORE * rows * cols
    factor = jnp.minimum(1.0, jnp.sqrt(f32(element_count)) / (jnp.sqrt(square_sum) + 1e-06))

    owner_hot = (new_host[None, :] == hosts[:, None]).astype(jnp.int32)
    source = jnp.sum(owner_hot * old_host[None, :], axis=1)

    tok_count, width = tokens.shape
    top = routes.shape[1]
    capacity = 3 * tok_count * top // (2 * host_count)
    place = ((old_host % Z) // SHARE * X + old_host // Z) * SHARE + old_host % SHARE
    route_place = jnp.sum(
        jnp.where(routes[:, :, None] == hosts[None, None, :], place[None, None, :], 0), axis=2
    ).T
    hits = route_place[None, :, :] == hosts[:, None, None]
    chosen = jnp.any(hits, axis=1)
    gate = jnp.sum(jnp.where(hits, route_weights.T[None, :, :], 0.0), axis=1)
    token_ids = jnp.arange(tok_count, dtype=jnp.int32)
    before = (token_ids[:, None] < token_ids[None, :]).astype(bf16)
    rank = jnp.dot(chosen.astype(bf16), before, preferred_element_type=f32)
    slot = jnp.where(chosen, rank, -1.0)
    slot_ids = jnp.arange(capacity, dtype=jnp.int32).astype(f32)
    taken = slot[:, None, :] == slot_ids[None, :, None]
    pick = taken.astype(bf16).reshape(-1, tok_count)
    outgoing = jnp.dot(pick, tokens, preferred_element_type=f32).astype(bf16)
    outgoing = outgoing.reshape(Y * CORE * X, SHARE * capacity, width)
    mix = jnp.where(taken, gate[:, None, :], 0.0).reshape(-1, tok_count)
    mix_high = mix.astype(bf16)
    mix_low = (mix - mix_high.astype(f32)).astype(bf16)
    outgoing, factor = lax.optimization_barrier((outgoing, factor))

    new_master, new_one, new_two = adamw(master, moment_one, moment_two, gradients, factor)
    gathered = lax.all_gather(new_master.astype(bf16), "z", axis=0, tiled=True)
    moments = jnp.stack([new_one.astype(bf16), new_two.astype(bf16)])
    quarter = rows // X
    moments = moments.reshape(2, X, quarter, cols).transpose(1, 0, 2, 3)
    received = swap(outgoing, PLANE)
    moments, received = lax.optimization_barrier((moments, received))
    moments = swap(moments, "x")
    moments = lax.all_gather(moments.reshape(-1, cols), "z", axis=0, tiled=True)

    planes = gathered.reshape(Z, rows, cols)
    plane_source = source.reshape(X, Z)[:, my_z]
    src_x, src_z = plane_source // Z, plane_source % Z
    to = [(my_x + shift) % X for shift in range(X)]
    held = [lax.dynamic_index_in_dim(planes, src_z[i], 0, False) for i in to]
    arrived = held[:1] + shifted(held[1:], X)
    back = (my_x - src_x[my_x]) % X
    moved_master = lax.select_n(back, *arrived)

    weights = swap(gathered.reshape(Y * CORE, SHARE * rows, cols), DP)
    weights = weights.reshape(Y * CORE, SHARE, rows, cols)
    hidden_units = cols // 3
    inputs = received.reshape(-1, SHARE, capacity, width)
    outs = []
    for j in range(SHARE):
        weight = weights[:, j].reshape(-1, cols)
        rows_in = inputs[:, j].reshape(-1, width)
        projected = jnp.dot(rows_in, weight[:, : 2 * hidden_units], preferred_element_type=f32)
        hidden = (jax.nn.silu(projected[:, :hidden_units]) * projected[:, hidden_units:]).astype(bf16)
        produced = lax.dot_general(
            hidden,
            weight[:, 2 * hidden_units :],
            (((1,), (1,)), ((), ())),
            preferred_element_type=f32,
        )
        outs.append(produced.astype(bf16).reshape(-1, capacity, width))
    results = jnp.stack(outs, axis=1).reshape(received.shape)
    returned = swap(results, PLANE).reshape(-1, width)
    contract = (((0,), (0,)), ((), ()))
    mixed = lax.dot_general(mix_high, returned, contract, preferred_element_type=f32)
    mixed += lax.dot_general(mix_low, returned, contract, preferred_element_type=f32)
    mixed = mixed.astype(bf16)

    pieces = moments.reshape(Z, X, 2, quarter, cols)
    held = [
        lax.dynamic_slice(pieces, (src_z[i], src_x[i], 0, 0, 0), (1, 1, 2, quarter, cols))[0, 0]
        for i in to
    ]
    arrived = jnp.stack(held[:1] + shifted(held[1:], X))
    order = (my_x - jnp.arange(X, dtype=jnp.int32)) % X
    arrived = jnp.take(arrived, order, axis=0)
    moved_moments = arrived.transpose(1, 0, 2, 3).reshape(2, rows, cols)
    moved = source[my_host] != my_host
    return (
        jnp.where(moved, moved_master.astype(f32), new_master)[None],
        jnp.where(moved, moved_moments[0].astype(f32), new_one)[None],
        jnp.where(moved, moved_moments[1].astype(f32), new_two)[None],
        mixed,
    )


def solution(mesh):
    fine = Mesh(mesh.devices.reshape(Y, CORE, X, Z), ("y", "c", "x", "z"))
    state = P(("x", "z"), DP, None)
    rows = P(("y", "c", "x", "z"), None)
    return jax.shard_map(
        per_device,
        mesh=fine,
        in_specs=(state, state, state, state, P(), P(), rows, rows, rows),
        out_specs=(state, state, state, rows),
        check_vma=False,
    )
```

```python
import jax
import jax.numpy as jnp
from jax import lax
from jax.experimental import pallas as pl
from jax.experimental.pallas import tpu as pltpu
from jax.sharding import Mesh, PartitionSpec as P

beta_one = 0.9
beta_two = 0.95
epsilon = 1e-08
learn_rate = 0.001
decay_rate = 0.1
step_count = 10

Y, CORE, X, Z = 4, 2, 4, 16
NEAR = 4
SLOTS = 10
DP = ("y", "c")
PLANE = ("y", "c", "x")
RING = ("far", "near")
SHARE = Z // (Y * CORE)
bf16, f32 = jnp.bfloat16, jnp.float32


def adamw(master, moment_one, moment_two, gradients, factor):
    scaled = gradients.astype(f32) * factor
    new_one = beta_one * moment_one + (1.0 - beta_one) * scaled
    new_two = beta_two * moment_two + (1.0 - beta_two) * scaled * scaled
    corrected_one = new_one / (1.0 - beta_one**step_count)
    corrected_two = new_two / (1.0 - beta_two**step_count)
    step_size = corrected_one / (jnp.sqrt(corrected_two) + epsilon) + decay_rate * master
    return (master - learn_rate * step_size, new_one, new_two)


def swap(array, axes):
    return lax.all_to_all(array, axes, split_axis=0, concat_axis=0, tiled=True)


def spread_squares(values, sent):
    value = values[...].astype(f32)
    sent[...] = jnp.full(sent.shape, jnp.sum(value * value), f32)


def spread_sum(values, sent):
    sent[...] = jnp.broadcast_to(jnp.sum(values[...], axis=0, keepdims=True), sent.shape)


def spread(kernel, operand, axes):
    return pl.pallas_call(
        kernel, out_shape=jax.ShapeDtypeStruct((lax.axis_size(axes), 1, 128), f32)
    )(operand)


PLANE_AT, GROUP_AT, SLOT_AT, BACK, MOVED, MY_X, OVER, PICK_AT, PLAN = 0, 4, 8, 12, 13, 14, 15, 16, 32


def make_plan(old_host, new_host, plan, source, target, rank):
    my_x = lax.axis_index("x")
    my_group = lax.axis_index("far")
    my_z = my_group * NEAR + lax.axis_index("near")

    @pl.loop(0, X * Z)
    def _(expert):
        source[new_host[expert]] = old_host[expert]
        target[old_host[expert]] = new_host[expert]

    for k in range(SLOTS):
        plan[PICK_AT + k] = 0
    over = jnp.int32(0)
    for group in range(Z // NEAR):

        def visit(place, count, group=group):
            host = (place // NEAR) * Z + group * NEAR + lax.rem(place, NEAR)
            leaves = target[host] != host
            rank[host] = count

            @pl.when(leaves & (my_group == group) & (count < SLOTS))
            def _():
                plan[PICK_AT + count] = place

            return count + leaves.astype(jnp.int32)

        count = lax.fori_loop(0, X * NEAR, visit, jnp.int32(0))
        over = jnp.maximum(over, (count > SLOTS).astype(jnp.int32))
    for shift in range(X):
        host = source[lax.rem(my_x + shift, X) * Z + my_z]
        plan[PLANE_AT + shift] = lax.rem(host, Z)
        plan[GROUP_AT + shift] = lax.rem(host, Z) // NEAR
        plan[SLOT_AT + shift] = jnp.minimum(rank[host], SLOTS - 1)
    mine = source[my_x * Z + my_z]
    plan[BACK] = lax.rem(my_x + X - mine // Z, X)
    plan[MOVED] = (mine != my_x * Z + my_z).astype(jnp.int32)
    plan[MY_X] = my_x
    plan[OVER] = over


def plan_of(old_host, new_host):
    scalars = pl.BlockSpec(memory_space=pltpu.SMEM)
    return pl.pallas_call(
        make_plan,
        out_shape=jax.ShapeDtypeStruct((PLAN,), jnp.int32),
        in_specs=[scalars, scalars],
        out_specs=scalars,
        scratch_shapes=[pltpu.SMEM((X * Z,), jnp.int32)] * 3,
    )(old_host, new_host)


def copy_picked(plan, *refs):
    half = len(refs) // 2
    for taken, kept in zip(refs[:half], refs[half:]):
        kept[...] = taken[...].reshape(kept.shape)


def pick_planes(plan, planes):
    rows, cols = planes.shape[1:]

    def take(shift):
        return pl.BlockSpec((1, rows, cols), lambda i, plan: (plan[PLANE_AT + shift], 0, 0))

    return pl.pallas_call(
        copy_picked,
        out_shape=[jax.ShapeDtypeStruct((rows, cols), bf16)] * X,
        grid_spec=pltpu.PrefetchScalarGridSpec(
            num_scalar_prefetch=1,
            grid=(1,),
            in_specs=[take(shift) for shift in range(X)],
            out_specs=[pl.BlockSpec((rows, cols), lambda i, plan: (0, 0))] * X,
        ),
    )(plan, *[planes] * X)


def pick_pieces(plan, pieces):
    rows, cols = pieces.shape[3:]
    block = (1, NEAR, 1, rows, cols)

    def take(shift):
        return pl.BlockSpec(
            block, lambda i, plan: (plan[GROUP_AT + shift], 0, plan[SLOT_AT + shift], 0, 0)
        )

    return pl.pallas_call(
        copy_picked,
        out_shape=[jax.ShapeDtypeStruct((NEAR, rows, cols), bf16)] * X,
        grid_spec=pltpu.PrefetchScalarGridSpec(
            num_scalar_prefetch=1,
            grid=(1,),
            in_specs=[take(shift) for shift in range(X)],
            out_specs=[pl.BlockSpec((NEAR, rows, cols), lambda i, plan: (0, 0, 0))] * X,
        ),
    )(plan, *[pieces] * X)


def compact(plan, pieces, slots):
    for k in range(SLOTS):
        slots[k] = pieces[plan[PICK_AT + k]]


def compacted(plan, pieces):
    return pl.pallas_call(
        compact,
        out_shape=jax.ShapeDtypeStruct((SLOTS,) + pieces.shape[1:], bf16),
        grid_spec=pltpu.PrefetchScalarGridSpec(
            num_scalar_prefetch=1,
            grid=(1,),
            in_specs=[pl.BlockSpec(pieces.shape, lambda i, plan: (0, 0, 0))],
            out_specs=pl.BlockSpec((SLOTS,) + pieces.shape[1:], lambda i, plan: (0, 0, 0)),
        ),
    )(plan, pieces)


def finish(plan, here, one, two, three, own_one, own_two, new_one, new_two):
    new_one[...] = own_one[...]
    new_two[...] = own_two[...]

    @pl.when(plan[MOVED] == 1)
    def _():
        for shift, quarter in enumerate((here, one, two, three)):
            at = lax.rem(plan[MY_X] + X - shift, X) * NEAR
            for near in range(NEAR):
                piece = quarter[near].astype(f32)
                half = piece.shape[0] // 2
                rows = pl.ds(pl.multiple_of((at + near) * half, half), half)
                new_one[rows] = piece[:half]
                new_two[rows] = piece[half:]


def finished(plan, arrived, own_one, own_two):
    whole = pl.BlockSpec(memory_space=pltpu.VMEM)
    return pl.pallas_call(
        finish,
        out_shape=[jax.ShapeDtypeStruct(own_one.shape, f32)] * 2,
        in_specs=[pl.BlockSpec(memory_space=pltpu.SMEM)] + [whole] * 6,
        out_specs=[whole] * 2,
    )(plan, *arrived, own_one, own_two)


def relocated_whole(old_host, new_host, own_one, own_two):
    rows, cols = own_one.shape
    quarter = rows // X
    hosts = jnp.arange(X * Z, dtype=jnp.int32)
    owner_hot = (new_host[None, :] == hosts[:, None]).astype(jnp.int32)
    source = jnp.sum(owner_hot * old_host[None, :], axis=1)
    my_x, my_z = lax.axis_index("x"), lax.axis_index(RING)
    plane_source = source.reshape(X, Z)[:, my_z]
    src_x, src_z = plane_source // Z, plane_source % Z
    moments = jnp.stack([own_one.astype(bf16), own_two.astype(bf16)])
    moments = swap(moments.reshape(2, X, quarter, cols).transpose(1, 0, 2, 3), "x")
    moments = lax.all_gather(moments.reshape(-1, cols), RING, axis=0, tiled=True)
    pieces = moments.reshape(Z, X, 2, quarter, cols)
    size = (1, 1, 2, quarter, cols)
    sent = [lax.dynamic_slice(pieces, (src_z[i], src_x[i], 0, 0, 0), size)[0, 0] for i in range(X)]
    arrived = swap(jnp.stack(sent), "x").transpose(1, 0, 2, 3).reshape(2, rows, cols)
    moved = plane_source[my_x] != my_x * Z + my_z
    return [
        jnp.where(moved, arrived[0].astype(f32), own_one),
        jnp.where(moved, arrived[1].astype(f32), own_two),
    ]


def shifted(blocks, size):
    return [
        lax.ppermute(block, "x", [(i, (i + shift) % size) for i in range(size)])
        for shift, block in enumerate(blocks, 1)
    ]


def per_device(
    master, moment_one, moment_two, gradients, old_host, new_host, tokens, routes, route_weights
):
    master, moment_one, moment_two, gradients = (
        item[0] for item in (master, moment_one, moment_two, gradients)
    )
    rows, cols = master.shape
    host_count = X * Z
    hosts = jnp.arange(host_count, dtype=jnp.int32)

    squares = swap(spread(spread_squares, gradients, PLANE), PLANE)
    squares = swap(spread(spread_sum, squares, RING), RING)
    square_sum = jnp.sum(squares[:, 0, 0])
    element_count = host_count * Y * CORE * rows * cols
    factor = jnp.minimum(1.0, jnp.sqrt(f32(element_count)) / (jnp.sqrt(square_sum) + 1e-06))

    plan = plan_of(old_host, new_host)

    tok_count, width = tokens.shape
    top = routes.shape[1]
    capacity = 3 * tok_count * top // (2 * host_count)
    place = ((old_host % Z) // SHARE * X + old_host // Z) * SHARE + old_host % SHARE
    route_place = jnp.sum(
        jnp.where(routes[:, :, None] == hosts[None, None, :], place[None, None, :], 0), axis=2
    ).T
    hits = route_place[None, :, :] == hosts[:, None, None]
    chosen = jnp.any(hits, axis=1)
    gate = jnp.sum(jnp.where(hits, route_weights.T[None, :, :], 0.0), axis=1)
    token_ids = jnp.arange(tok_count, dtype=jnp.int32)
    before = (token_ids[:, None] < token_ids[None, :]).astype(bf16)
    rank = jnp.dot(chosen.astype(bf16), before, preferred_element_type=f32)
    slot = jnp.where(chosen, rank, -1.0)
    slot_ids = jnp.arange(capacity, dtype=jnp.int32).astype(f32)
    taken = slot[:, None, :] == slot_ids[None, :, None]
    pick = taken.astype(bf16).reshape(-1, tok_count)
    outgoing = jnp.dot(pick, tokens, preferred_element_type=f32).astype(bf16)
    outgoing = outgoing.reshape(Y * CORE * X, SHARE * capacity, width)
    mix = jnp.where(taken, gate[:, None, :], 0.0).reshape(-1, tok_count)
    mix_high = mix.astype(bf16)
    mix_low = (mix - mix_high.astype(f32)).astype(bf16)
    mix_both = jnp.concatenate([mix_high, mix_low], axis=1)
    outgoing, factor = lax.optimization_barrier((outgoing, factor))

    new_master, new_one, new_two = adamw(master, moment_one, moment_two, gradients, factor)
    gathered = lax.all_gather(new_master.astype(bf16), RING, axis=0, tiled=True)
    received = swap(outgoing, PLANE)
    piece = rows // (X * NEAR)
    pieces = jnp.concatenate(
        [item.astype(bf16).reshape(-1, piece, cols) for item in (new_one, new_two)], axis=1
    )
    pieces, received = lax.optimization_barrier((pieces, received))
    pieces = compacted(plan, swap(pieces, ("x", "near")))
    pieces = lax.all_gather(pieces.reshape(-1, cols), RING, axis=0, tiled=True)

    held = pick_planes(plan, gathered.reshape(Z, rows, cols))
    gathered, held = lax.optimization_barrier((gathered, held))
    masters = [held[0]] + shifted(held[1:], X)

    weights = swap(gathered.reshape(Y * CORE, SHARE * rows, cols), DP)
    weights, masters = lax.optimization_barrier((weights, masters))
    moved = plan[MOVED] == 1
    moved_master = lax.select_n(plan[BACK], *masters).astype(f32)
    weights = weights.reshape(Y * CORE, SHARE, rows, cols)
    hidden_units = cols // 3
    inputs = received.reshape(-1, SHARE, capacity, width)
    outs = []
    for j in range(SHARE):
        weight = weights[:, j].reshape(-1, cols)
        rows_in = inputs[:, j].reshape(-1, width)
        projected = jnp.dot(rows_in, weight[:, : 2 * hidden_units], preferred_element_type=f32)
        hidden = (jax.nn.silu(projected[:, :hidden_units]) * projected[:, hidden_units:]).astype(bf16)
        produced = lax.dot_general(
            hidden,
            weight[:, 2 * hidden_units :],
            (((1,), (1,)), ((), ())),
            preferred_element_type=f32,
        )
        outs.append(produced.astype(bf16).reshape(-1, capacity, width))
    results = jnp.stack(outs, axis=1).reshape(received.shape)
    returned = swap(results, PLANE).reshape(-1, width)
    contract = (((0,), (0,)), ((), ()))
    mixed = lax.dot_general(mix_both, returned, contract, preferred_element_type=f32)
    mixed = (mixed[:tok_count] + mixed[tok_count:]).astype(bf16)

    held = pick_pieces(plan, pieces.reshape(Z // NEAR, NEAR, SLOTS, 2 * piece, cols))
    moments = finished(plan, [held[0]] + shifted(held[1:], X), new_one, new_two)
    moments = lax.cond(
        plan[OVER] == 1,
        lambda: relocated_whole(old_host, new_host, new_one, new_two),
        lambda: list(moments),
    )
    return (
        jnp.where(moved, moved_master, new_master)[None],
        moments[0][None],
        moments[1][None],
        mixed,
    )


def solution(mesh):
    fine = Mesh(mesh.devices.reshape(Y, CORE, X, Z // NEAR, NEAR), PLANE + RING)
    state = P(("x",) + RING, DP, None)
    rows = P(PLANE + RING, None)
    return jax.shard_map(
        per_device,
        mesh=fine,
        in_specs=(state, state, state, state, P(), P(), rows, rows, rows),
        out_specs=(state, state, state, rows),
        check_vma=False,
    )
```

```python
import jax
import jax.numpy as jnp
from jax import lax
from jax.experimental import pallas as pl
from jax.experimental.pallas import tpu as pltpu
from jax.sharding import Mesh, PartitionSpec as P

beta_one = 0.9
beta_two = 0.95
epsilon = 1e-08
learn_rate = 0.001
decay_rate = 0.1
step_count = 10

Y, CORE, X, Z = 4, 2, 4, 16
NEAR = 2
SLOTS = 6
DP = ("y", "c")
PLANE = ("y", "c", "x")
RING = ("far", "near")
SHARE = Z // (Y * CORE)
bf16, f32 = jnp.bfloat16, jnp.float32


def adamw(master, moment_one, moment_two, gradients, factor):
    scaled = gradients.astype(f32) * factor
    new_one = beta_one * moment_one + (1.0 - beta_one) * scaled
    new_two = beta_two * moment_two + (1.0 - beta_two) * scaled * scaled
    corrected_one = new_one / (1.0 - beta_one**step_count)
    corrected_two = new_two / (1.0 - beta_two**step_count)
    step_size = corrected_one / (jnp.sqrt(corrected_two) + epsilon) + decay_rate * master
    return (master - learn_rate * step_size, new_one, new_two)


def swap(array, axes):
    return lax.all_to_all(array, axes, split_axis=0, concat_axis=0, tiled=True)


def spread_squares(values, sent):
    value = values[...].astype(f32)
    sent[...] = jnp.full(sent.shape, jnp.sum(value * value), f32)


def spread_sum(values, sent):
    sent[...] = jnp.broadcast_to(jnp.sum(values[...], axis=0, keepdims=True), sent.shape)


def spread(kernel, operand, axes):
    return pl.pallas_call(
        kernel, out_shape=jax.ShapeDtypeStruct((lax.axis_size(axes), 1, 128), f32)
    )(operand)


PLANE_AT, GROUP_AT, SLOT_AT, BACK, MOVED, MY_X, OVER, PICK_AT, PLAN = 0, 4, 8, 12, 13, 14, 15, 16, 32


def make_plan(old_host, new_host, plan, source, target, rank):
    my_x = lax.axis_index("x")
    my_group = lax.axis_index("far")
    my_z = my_group * NEAR + lax.axis_index("near")

    @pl.loop(0, X * Z)
    def _(expert):
        source[new_host[expert]] = old_host[expert]
        target[old_host[expert]] = new_host[expert]

    for k in range(SLOTS):
        plan[PICK_AT + k] = 0
    over = jnp.int32(0)
    for group in range(Z // NEAR):

        def visit(place, count, group=group):
            host = (place // NEAR) * Z + group * NEAR + lax.rem(place, NEAR)
            leaves = target[host] != host
            rank[host] = count

            @pl.when(leaves & (my_group == group) & (count < SLOTS))
            def _():
                plan[PICK_AT + count] = place

            return count + leaves.astype(jnp.int32)

        count = lax.fori_loop(0, X * NEAR, visit, jnp.int32(0))
        over = jnp.maximum(over, (count > SLOTS).astype(jnp.int32))
    for shift in range(X):
        host = source[lax.rem(my_x + shift, X) * Z + my_z]
        plan[PLANE_AT + shift] = lax.rem(host, Z)
        plan[GROUP_AT + shift] = lax.rem(host, Z) // NEAR
        plan[SLOT_AT + shift] = jnp.minimum(rank[host], SLOTS - 1)
    mine = source[my_x * Z + my_z]
    plan[BACK] = lax.rem(my_x + X - mine // Z, X)
    plan[MOVED] = (mine != my_x * Z + my_z).astype(jnp.int32)
    plan[MY_X] = my_x
    plan[OVER] = over


def plan_of(old_host, new_host):
    scalars = pl.BlockSpec(memory_space=pltpu.SMEM)
    return pl.pallas_call(
        make_plan,
        out_shape=jax.ShapeDtypeStruct((PLAN,), jnp.int32),
        in_specs=[scalars, scalars],
        out_specs=scalars,
        scratch_shapes=[pltpu.SMEM((X * Z,), jnp.int32)] * 3,
    )(old_host, new_host)


def copy_picked(plan, *refs):
    half = len(refs) // 2
    for taken, kept in zip(refs[:half], refs[half:]):
        kept[...] = taken[...].reshape(kept.shape)


def pick_planes(plan, planes):
    rows, cols = planes.shape[1:]

    def take(shift):
        return pl.BlockSpec((1, rows, cols), lambda i, plan: (plan[PLANE_AT + shift], 0, 0))

    return pl.pallas_call(
        copy_picked,
        out_shape=[jax.ShapeDtypeStruct((rows, cols), bf16)] * X,
        grid_spec=pltpu.PrefetchScalarGridSpec(
            num_scalar_prefetch=1,
            grid=(1,),
            in_specs=[take(shift) for shift in range(X)],
            out_specs=[pl.BlockSpec((rows, cols), lambda i, plan: (0, 0))] * X,
        ),
    )(plan, *[planes] * X)


def pick_pieces(plan, pieces):
    rows, cols = pieces.shape[3:]
    block = (1, NEAR, 1, rows, cols)

    def take(shift):
        return pl.BlockSpec(
            block, lambda i, plan: (plan[GROUP_AT + shift], 0, plan[SLOT_AT + shift], 0, 0)
        )

    return pl.pallas_call(
        copy_picked,
        out_shape=[jax.ShapeDtypeStruct((NEAR, rows, cols), bf16)] * X,
        grid_spec=pltpu.PrefetchScalarGridSpec(
            num_scalar_prefetch=1,
            grid=(1,),
            in_specs=[take(shift) for shift in range(X)],
            out_specs=[pl.BlockSpec((NEAR, rows, cols), lambda i, plan: (0, 0, 0))] * X,
        ),
    )(plan, *[pieces] * X)


def compact(plan, pieces, slots):
    for k in range(SLOTS):
        slots[k] = pieces[plan[PICK_AT + k]]


def compacted(plan, pieces):
    return pl.pallas_call(
        compact,
        out_shape=jax.ShapeDtypeStruct((SLOTS,) + pieces.shape[1:], bf16),
        grid_spec=pltpu.PrefetchScalarGridSpec(
            num_scalar_prefetch=1,
            grid=(1,),
            in_specs=[pl.BlockSpec(pieces.shape, lambda i, plan: (0, 0, 0))],
            out_specs=pl.BlockSpec((SLOTS,) + pieces.shape[1:], lambda i, plan: (0, 0, 0)),
        ),
    )(plan, pieces)


def finish(plan, here, one, two, three, own_one, own_two, new_one, new_two):
    new_one[...] = own_one[...]
    new_two[...] = own_two[...]

    @pl.when(plan[MOVED] == 1)
    def _():
        for shift, quarter in enumerate((here, one, two, three)):
            at = lax.rem(plan[MY_X] + X - shift, X) * NEAR
            for near in range(NEAR):
                piece = quarter[near].astype(f32)
                half = piece.shape[0] // 2
                rows = pl.ds(pl.multiple_of((at + near) * half, half), half)
                new_one[rows] = piece[:half]
                new_two[rows] = piece[half:]


def finished(plan, arrived, own_one, own_two):
    whole = pl.BlockSpec(memory_space=pltpu.VMEM)
    return pl.pallas_call(
        finish,
        out_shape=[jax.ShapeDtypeStruct(own_one.shape, f32)] * 2,
        in_specs=[pl.BlockSpec(memory_space=pltpu.SMEM)] + [whole] * 6,
        out_specs=[whole] * 2,
    )(plan, *arrived, own_one, own_two)


def relocated_whole(old_host, new_host, own_one, own_two):
    rows, cols = own_one.shape
    quarter = rows // X
    hosts = jnp.arange(X * Z, dtype=jnp.int32)
    owner_hot = (new_host[None, :] == hosts[:, None]).astype(jnp.int32)
    source = jnp.sum(owner_hot * old_host[None, :], axis=1)
    my_x, my_z = lax.axis_index("x"), lax.axis_index(RING)
    plane_source = source.reshape(X, Z)[:, my_z]
    src_x, src_z = plane_source // Z, plane_source % Z
    moments = jnp.stack([own_one.astype(bf16), own_two.astype(bf16)])
    moments = swap(moments.reshape(2, X, quarter, cols).transpose(1, 0, 2, 3), "x")
    moments = lax.all_gather(moments.reshape(-1, cols), RING, axis=0, tiled=True)
    pieces = moments.reshape(Z, X, 2, quarter, cols)
    size = (1, 1, 2, quarter, cols)
    sent = [lax.dynamic_slice(pieces, (src_z[i], src_x[i], 0, 0, 0), size)[0, 0] for i in range(X)]
    arrived = swap(jnp.stack(sent), "x").transpose(1, 0, 2, 3).reshape(2, rows, cols)
    moved = plane_source[my_x] != my_x * Z + my_z
    return [
        jnp.where(moved, arrived[0].astype(f32), own_one),
        jnp.where(moved, arrived[1].astype(f32), own_two),
    ]


def expert_layer(rows, weights, outs):
    weight = weights[...].reshape(-1, weights.shape[-1])
    units = weight.shape[1] // 3
    projected = jnp.dot(rows[0], weight[:, : 2 * units], preferred_element_type=f32)
    hidden = (jax.nn.silu(projected[:, :units]) * projected[:, units:]).astype(bf16)
    produced = lax.dot_general(
        hidden, weight[:, 2 * units :], (((1,), (1,)), ((), ())), preferred_element_type=f32
    )
    outs[...] = produced.reshape(outs.shape).astype(bf16)


def experts(rows, weights, capacity):
    shares, row_count, width = rows.shape
    shards, _, shard_rows, cols = weights.shape
    parts = 2
    part = row_count // parts
    return pl.pallas_call(
        expert_layer,
        out_shape=jax.ShapeDtypeStruct((row_count // capacity, shares, capacity, width), bf16),
        grid=(shares, parts),
        in_specs=[
            pl.BlockSpec((1, part, width), lambda j, i: (j, i, 0)),
            pl.BlockSpec((shards, 1, shard_rows, cols), lambda j, i: (0, j, 0, 0)),
        ],
        out_specs=pl.BlockSpec((part // capacity, 1, capacity, width), lambda j, i: (i, j, 0, 0)),
        compiler_params=pltpu.CompilerParams(vmem_limit_bytes=48 * 2**20),
        cost_estimate=pl.CostEstimate(
            flops=2 * shares * row_count * width * cols,
            bytes_accessed=2 * (weights.size + 2 * rows.size),
            transcendentals=shares * row_count * cols // 3,
        ),
    )(rows, weights)


def shifted(blocks, size):
    return [
        lax.ppermute(block, "x", [(i, (i + shift) % size) for i in range(size)])
        for shift, block in enumerate(blocks, 1)
    ]


def per_device(
    master, moment_one, moment_two, gradients, old_host, new_host, tokens, routes, route_weights
):
    master, moment_one, moment_two, gradients = (
        item[0] for item in (master, moment_one, moment_two, gradients)
    )
    rows, cols = master.shape
    host_count = X * Z
    hosts = jnp.arange(host_count, dtype=jnp.int32)

    squares = swap(spread(spread_squares, gradients, PLANE), PLANE)
    squares = swap(spread(spread_sum, squares, RING), RING)
    square_sum = jnp.sum(squares[:, 0, 0])
    element_count = host_count * Y * CORE * rows * cols
    factor = jnp.minimum(1.0, jnp.sqrt(f32(element_count)) / (jnp.sqrt(square_sum) + 1e-06))

    plan = plan_of(old_host, new_host)

    tok_count, width = tokens.shape
    top = routes.shape[1]
    capacity = 3 * tok_count * top // (2 * host_count)
    place = ((old_host % Z) // SHARE * X + old_host // Z) * SHARE + old_host % SHARE
    route_place = jnp.sum(
        jnp.where(routes[:, :, None] == hosts[None, None, :], place[None, None, :], 0), axis=2
    ).T
    hits = route_place[None, :, :] == hosts[:, None, None]
    chosen = jnp.any(hits, axis=1)
    gate = jnp.sum(jnp.where(hits, route_weights.T[None, :, :], 0.0), axis=1)
    token_ids = jnp.arange(tok_count, dtype=jnp.int32)
    before = (token_ids[:, None] < token_ids[None, :]).astype(bf16)
    rank = jnp.dot(chosen.astype(bf16), before, preferred_element_type=f32)
    slot = jnp.where(chosen, rank, -1.0)
    slot_ids = jnp.arange(capacity, dtype=jnp.int32).astype(f32)
    taken = slot[:, None, :] == slot_ids[None, :, None]
    pick = taken.astype(bf16).reshape(-1, tok_count)
    outgoing = jnp.dot(pick, tokens, preferred_element_type=f32).astype(bf16)
    outgoing = outgoing.reshape(Y * CORE * X, SHARE * capacity, width)
    mix = jnp.where(taken, gate[:, None, :], 0.0).reshape(-1, tok_count)
    mix_high = mix.astype(bf16)
    mix_low = (mix - mix_high.astype(f32)).astype(bf16)
    mix_both = jnp.concatenate([mix_high, mix_low], axis=1)
    outgoing, factor = lax.optimization_barrier((outgoing, factor))

    new_master, new_one, new_two = adamw(master, moment_one, moment_two, gradients, factor)
    gathered = lax.all_gather(new_master.astype(bf16), RING, axis=0, tiled=True)
    received = swap(outgoing, PLANE)
    piece = rows // (X * NEAR)
    pieces = jnp.concatenate(
        [item.astype(bf16).reshape(-1, piece, cols) for item in (new_one, new_two)], axis=1
    )
    pieces, received = lax.optimization_barrier((pieces, received))
    pieces = compacted(plan, swap(pieces, ("x", "near")))
    pieces = lax.all_gather(pieces.reshape(-1, cols), RING, axis=0, tiled=True)

    held = pick_planes(plan, gathered.reshape(Z, rows, cols))
    masters = [held[0]] + shifted(held[1:], X)

    weights = swap(gathered.reshape(Y * CORE, SHARE * rows, cols), DP)
    weights, masters = lax.optimization_barrier((weights, masters))
    moved = plan[MOVED] == 1
    moved_master = lax.select_n(plan[BACK], *masters).astype(f32)
    weights = weights.reshape(Y * CORE, SHARE, rows, cols)
    inputs = received.reshape(-1, SHARE, capacity, width).transpose(1, 0, 2, 3)
    results = experts(inputs.reshape(SHARE, -1, width), weights, capacity).reshape(received.shape)
    results, late_plan = lax.optimization_barrier((results, plan))
    returned = swap(results, PLANE).reshape(-1, width)

    held = pick_pieces(late_plan, pieces.reshape(Z // NEAR, NEAR, SLOTS, 2 * piece, cols))
    moments = finished(plan, [held[0]] + shifted(held[1:], X), new_one, new_two)
    returned, moments = lax.optimization_barrier((returned, list(moments)))
    moments = lax.cond(
        plan[OVER] == 1,
        lambda: relocated_whole(old_host, new_host, new_one, new_two),
        lambda: moments,
    )

    contract = (((0,), (0,)), ((), ()))
    mixed = lax.dot_general(mix_both, returned, contract, preferred_element_type=f32)
    mixed = (mixed[:tok_count] + mixed[tok_count:]).astype(bf16)
    return (
        jnp.where(moved, moved_master, new_master)[None],
        moments[0][None],
        moments[1][None],
        mixed,
    )


def solution(mesh):
    fine = Mesh(mesh.devices.reshape(Y, CORE, X, Z // NEAR, NEAR), PLANE + RING)
    state = P(("x",) + RING, DP, None)
    rows = P(PLANE + RING, None)
    return jax.shard_map(
        per_device,
        mesh=fine,
        in_specs=(state, state, state, state, P(), P(), rows, rows, rows),
        out_specs=(state, state, state, rows),
        check_vma=False,
    )
```

```python
import jax
import jax.numpy as jnp
from jax import lax
from jax.experimental import pallas as pl
from jax.experimental.pallas import tpu as pltpu
from jax.sharding import Mesh, PartitionSpec as P

beta_one = 0.9
beta_two = 0.95
epsilon = 1e-08
learn_rate = 0.001
decay_rate = 0.1
step_count = 10

Y, CORE, X, Z = 4, 2, 4, 16
NEAR = 2
SLOTS = 6
DP = ("y", "c")
PLANE = ("y", "c", "x")
RING = ("far", "near")
SHARE = Z // (Y * CORE)
bf16, f32 = jnp.bfloat16, jnp.float32


def adamw(master, moment_one, moment_two, gradients, factor):
    scaled = gradients.astype(f32) * factor
    new_one = beta_one * moment_one + (1.0 - beta_one) * scaled
    new_two = beta_two * moment_two + (1.0 - beta_two) * scaled * scaled
    corrected_one = new_one / (1.0 - beta_one**step_count)
    corrected_two = new_two / (1.0 - beta_two**step_count)
    step_size = corrected_one / (jnp.sqrt(corrected_two) + epsilon) + decay_rate * master
    return (master - learn_rate * step_size, new_one, new_two)


def swap(array, axes):
    return lax.all_to_all(array, axes, split_axis=0, concat_axis=0, tiled=True)


def limit(mebibytes):
    return pltpu.CompilerParams(vmem_limit_bytes=mebibytes * 2**20)


def spread_squares(values, sent):
    value = values[...].astype(f32)
    sent[...] = jnp.full(sent.shape, jnp.sum(value * value), f32)


def spread_sum(values, sent):
    sent[...] = jnp.broadcast_to(jnp.sum(values[...], axis=0, keepdims=True), sent.shape)


def spread(kernel, operand, axes):
    return pl.pallas_call(
        kernel,
        out_shape=jax.ShapeDtypeStruct((lax.axis_size(axes), 1, 128), f32),
        compiler_params=limit(2),
    )(operand)


PLANE_AT, GROUP_AT, SLOT_AT, BACK, MOVED, MY_X, OVER, PICK_AT, PLAN = 0, 4, 8, 12, 13, 14, 15, 16, 32


def make_plan(old_host, new_host, plan, source, target, rank):
    my_x = lax.axis_index("x")
    my_group = lax.axis_index("far")
    my_z = my_group * NEAR + lax.axis_index("near")

    @pl.loop(0, X * Z)
    def _(expert):
        source[new_host[expert]] = old_host[expert]
        target[old_host[expert]] = new_host[expert]

    for k in range(SLOTS):
        plan[PICK_AT + k] = 0
    over = jnp.int32(0)
    for group in range(Z // NEAR):

        def visit(place, count, group=group):
            host = (place // NEAR) * Z + group * NEAR + lax.rem(place, NEAR)
            leaves = target[host] != host
            rank[host] = count

            @pl.when(leaves & (my_group == group) & (count < SLOTS))
            def _():
                plan[PICK_AT + count] = place

            return count + leaves.astype(jnp.int32)

        count = lax.fori_loop(0, X * NEAR, visit, jnp.int32(0))
        over = jnp.maximum(over, (count > SLOTS).astype(jnp.int32))
    for shift in range(X):
        host = source[lax.rem(my_x + shift, X) * Z + my_z]
        plan[PLANE_AT + shift] = lax.rem(host, Z)
        plan[GROUP_AT + shift] = lax.rem(host, Z) // NEAR
        plan[SLOT_AT + shift] = jnp.minimum(rank[host], SLOTS - 1)
    mine = source[my_x * Z + my_z]
    plan[BACK] = lax.rem(my_x + X - mine // Z, X)
    plan[MOVED] = (mine != my_x * Z + my_z).astype(jnp.int32)
    plan[MY_X] = my_x
    plan[OVER] = over


def plan_of(old_host, new_host):
    scalars = pl.BlockSpec(memory_space=pltpu.SMEM)
    return pl.pallas_call(
        make_plan,
        out_shape=jax.ShapeDtypeStruct((PLAN,), jnp.int32),
        in_specs=[scalars, scalars],
        out_specs=scalars,
        scratch_shapes=[pltpu.SMEM((X * Z,), jnp.int32)] * 3,
        compiler_params=limit(1),
    )(old_host, new_host)


def copy_picked(plan, *refs):
    half = len(refs) // 2
    for taken, kept in zip(refs[:half], refs[half:]):
        kept[...] = taken[...].reshape(kept.shape)


def pick_planes(plan, planes):
    rows, cols = planes.shape[1:]

    def take(shift):
        return pl.BlockSpec((1, rows, cols), lambda i, plan: (plan[PLANE_AT + shift], 0, 0))

    return pl.pallas_call(
        copy_picked,
        out_shape=[jax.ShapeDtypeStruct((rows, cols), bf16)] * X,
        grid_spec=pltpu.PrefetchScalarGridSpec(
            num_scalar_prefetch=1,
            grid=(1,),
            in_specs=[take(shift) for shift in range(X)],
            out_specs=[pl.BlockSpec((rows, cols), lambda i, plan: (0, 0))] * X,
        ),
        compiler_params=limit(60),
    )(plan, *[planes] * X)


def pick_pieces(plan, pieces):
    rows, cols = pieces.shape[3:]
    block = (1, NEAR, 1, rows, cols)

    def take(shift):
        return pl.BlockSpec(
            block, lambda i, plan: (plan[GROUP_AT + shift], 0, plan[SLOT_AT + shift], 0, 0)
        )

    return pl.pallas_call(
        copy_picked,
        out_shape=[jax.ShapeDtypeStruct((NEAR, rows, cols), bf16)] * X,
        grid_spec=pltpu.PrefetchScalarGridSpec(
            num_scalar_prefetch=1,
            grid=(1,),
            in_specs=[take(shift) for shift in range(X)],
            out_specs=[pl.BlockSpec((NEAR, rows, cols), lambda i, plan: (0, 0, 0))] * X,
        ),
        compiler_params=limit(60),
    )(plan, *[pieces] * X)


def compact(plan, pieces, slots):
    for k in range(SLOTS):
        slots[k] = pieces[plan[PICK_AT + k]]


def compacted(plan, pieces):
    return pl.pallas_call(
        compact,
        out_shape=jax.ShapeDtypeStruct((SLOTS,) + pieces.shape[1:], bf16),
        grid_spec=pltpu.PrefetchScalarGridSpec(
            num_scalar_prefetch=1,
            grid=(1,),
            in_specs=[pl.BlockSpec(pieces.shape, lambda i, plan: (0, 0, 0))],
            out_specs=pl.BlockSpec((SLOTS,) + pieces.shape[1:], lambda i, plan: (0, 0, 0)),
        ),
        compiler_params=limit(4),
    )(plan, pieces)


def finish(plan, here, one, two, three, own_one, own_two, new_one, new_two):
    new_one[...] = own_one[...]
    new_two[...] = own_two[...]

    @pl.when(plan[MOVED] == 1)
    def _():
        for shift, quarter in enumerate((here, one, two, three)):
            at = lax.rem(plan[MY_X] + X - shift, X) * NEAR
            for near in range(NEAR):
                piece = quarter[near].astype(f32)
                half = piece.shape[0] // 2
                rows = pl.ds(pl.multiple_of((at + near) * half, half), half)
                new_one[rows] = piece[:half]
                new_two[rows] = piece[half:]


def finished(plan, arrived, own_one, own_two):
    whole = pl.BlockSpec(memory_space=pltpu.VMEM)
    return pl.pallas_call(
        finish,
        out_shape=[jax.ShapeDtypeStruct(own_one.shape, f32)] * 2,
        in_specs=[pl.BlockSpec(memory_space=pltpu.SMEM)] + [whole] * 6,
        out_specs=[whole] * 2,
        compiler_params=limit(8),
    )(plan, *arrived, own_one, own_two)


def relocated_whole(old_host, new_host, own_one, own_two):
    rows, cols = own_one.shape
    quarter = rows // X
    hosts = jnp.arange(X * Z, dtype=jnp.int32)
    owner_hot = (new_host[None, :] == hosts[:, None]).astype(jnp.int32)
    source = jnp.sum(owner_hot * old_host[None, :], axis=1)
    my_x, my_z = lax.axis_index("x"), lax.axis_index(RING)
    plane_source = source.reshape(X, Z)[:, my_z]
    src_x, src_z = plane_source // Z, plane_source % Z
    moments = jnp.stack([own_one.astype(bf16), own_two.astype(bf16)])
    moments = swap(moments.reshape(2, X, quarter, cols).transpose(1, 0, 2, 3), "x")
    moments = lax.all_gather(moments.reshape(-1, cols), RING, axis=0, tiled=True)
    pieces = moments.reshape(Z, X, 2, quarter, cols)
    size = (1, 1, 2, quarter, cols)
    sent = [lax.dynamic_slice(pieces, (src_z[i], src_x[i], 0, 0, 0), size)[0, 0] for i in range(X)]
    arrived = swap(jnp.stack(sent), "x").transpose(1, 0, 2, 3).reshape(2, rows, cols)
    moved = plane_source[my_x] != my_x * Z + my_z
    return [
        jnp.where(moved, arrived[0].astype(f32), own_one),
        jnp.where(moved, arrived[1].astype(f32), own_two),
    ]


def expert_layer(rows, weights, outs):
    weight = weights[...].reshape(-1, weights.shape[-1])
    units = weight.shape[1] // 3
    projected = jnp.dot(rows[0], weight[:, : 2 * units], preferred_element_type=f32)
    hidden = (jax.nn.silu(projected[:, :units]) * projected[:, units:]).astype(bf16)
    produced = lax.dot_general(
        hidden, weight[:, 2 * units :], (((1,), (1,)), ((), ())), preferred_element_type=f32
    )
    outs[...] = produced.reshape(outs.shape).astype(bf16)


def experts(rows, weights, capacity):
    shares, row_count, width = rows.shape
    shards, _, shard_rows, cols = weights.shape
    return pl.pallas_call(
        expert_layer,
        out_shape=jax.ShapeDtypeStruct((row_count // capacity, shares, capacity, width), bf16),
        grid=(shares,),
        in_specs=[
            pl.BlockSpec((1, row_count, width), lambda j: (j, 0, 0)),
            pl.BlockSpec((shards, 1, shard_rows, cols), lambda j: (0, j, 0, 0)),
        ],
        out_specs=pl.BlockSpec((row_count // capacity, 1, capacity, width), lambda j: (0, j, 0, 0)),
        compiler_params=limit(30),
        cost_estimate=pl.CostEstimate(
            flops=2 * shares * row_count * width * cols,
            bytes_accessed=2 * (weights.size + 2 * rows.size),
            transcendentals=shares * row_count * cols // 3,
        ),
    )(rows, weights)


def shifted(blocks, size):
    return [
        lax.ppermute(block, "x", [(i, (i + shift) % size) for i in range(size)])
        for shift, block in enumerate(blocks, 1)
    ]


def per_device(
    master, moment_one, moment_two, gradients, old_host, new_host, tokens, routes, route_weights
):
    master, moment_one, moment_two, gradients = (
        item[0] for item in (master, moment_one, moment_two, gradients)
    )
    rows, cols = master.shape
    host_count = X * Z
    hosts = jnp.arange(host_count, dtype=jnp.int32)

    squares = swap(spread(spread_squares, gradients, PLANE), PLANE)
    squares = swap(spread(spread_sum, squares, RING), RING)
    square_sum = jnp.sum(squares[:, 0, 0])
    element_count = host_count * Y * CORE * rows * cols
    factor = jnp.minimum(1.0, jnp.sqrt(f32(element_count)) / (jnp.sqrt(square_sum) + 1e-06))

    plan = plan_of(old_host, new_host)

    tok_count, width = tokens.shape
    top = routes.shape[1]
    capacity = 3 * tok_count * top // (2 * host_count)
    place = ((old_host % Z) // SHARE * X + old_host // Z) * SHARE + old_host % SHARE
    route_place = jnp.sum(
        jnp.where(routes[:, :, None] == hosts[None, None, :], place[None, None, :], 0), axis=2
    ).T
    hits = route_place[None, :, :] == hosts[:, None, None]
    chosen = jnp.any(hits, axis=1)
    gate = jnp.sum(jnp.where(hits, route_weights.T[None, :, :], 0.0), axis=1)
    token_ids = jnp.arange(tok_count, dtype=jnp.int32)
    before = (token_ids[:, None] < token_ids[None, :]).astype(bf16)
    rank = jnp.dot(chosen.astype(bf16), before, preferred_element_type=f32)
    slot = jnp.where(chosen, rank, -1.0)
    slot_ids = jnp.arange(capacity, dtype=jnp.int32).astype(f32)
    taken = slot[:, None, :] == slot_ids[None, :, None]
    pick = taken.astype(bf16).reshape(-1, tok_count)
    outgoing = jnp.dot(pick, tokens, preferred_element_type=f32).astype(bf16)
    outgoing = outgoing.reshape(Y * CORE * X, SHARE * capacity, width)
    mix = jnp.where(taken, gate[:, None, :], 0.0).reshape(-1, tok_count)
    mix_high = mix.astype(bf16)
    mix_low = (mix - mix_high.astype(f32)).astype(bf16)
    mix_both = jnp.concatenate([mix_high, mix_low], axis=1)
    outgoing, factor = lax.optimization_barrier((outgoing, factor))

    new_master, new_one, new_two = adamw(master, moment_one, moment_two, gradients, factor)
    new_master, new_one, new_two, rounded = lax.optimization_barrier(
        (new_master, new_one, new_two, new_master.astype(bf16))
    )
    gathered = lax.all_gather(rounded, RING, axis=0, tiled=True)
    piece = rows // (X * NEAR)
    pieces = jnp.concatenate(
        [item.astype(bf16).reshape(-1, piece, cols) for item in (new_one, new_two)], axis=1
    )
    pieces, outgoing = lax.optimization_barrier((swap(pieces, ("x", "near")), outgoing))
    received = swap(outgoing, PLANE)
    pieces = compacted(plan, pieces)
    pieces = lax.all_gather(pieces.reshape(-1, cols), RING, axis=0, tiled=True)

    held = pick_planes(plan, gathered.reshape(Z, rows, cols))
    masters = [held[0]] + shifted(held[1:], X)

    weights = swap(gathered.reshape(Y * CORE, SHARE * rows, cols), DP)
    weights, masters = lax.optimization_barrier((weights, masters))
    moved = plan[MOVED] == 1
    moved_master = lax.select_n(plan[BACK], *masters).astype(f32)
    weights = weights.reshape(Y * CORE, SHARE, rows, cols)
    inputs = received.reshape(-1, SHARE, capacity, width).transpose(1, 0, 2, 3)
    results = experts(inputs.reshape(SHARE, -1, width), weights, capacity).reshape(received.shape)
    results, late_plan = lax.optimization_barrier((results, plan))
    returned = swap(results, PLANE).reshape(-1, width)

    held = pick_pieces(late_plan, pieces.reshape(Z // NEAR, NEAR, SLOTS, 2 * piece, cols))
    moments = finished(plan, [held[0]] + shifted(held[1:], X), new_one, new_two)
    returned, moments = lax.optimization_barrier((returned, list(moments)))
    moments = lax.cond(
        plan[OVER] == 1,
        lambda: relocated_whole(old_host, new_host, new_one, new_two),
        lambda: moments,
    )

    contract = (((0,), (0,)), ((), ()))
    mixed = lax.dot_general(mix_both, returned, contract, preferred_element_type=f32)
    mixed = (mixed[:tok_count] + mixed[tok_count:]).astype(bf16)
    return (
        jnp.where(moved, moved_master, new_master)[None],
        moments[0][None],
        moments[1][None],
        mixed,
    )


def solution(mesh):
    fine = Mesh(mesh.devices.reshape(Y, CORE, X, Z // NEAR, NEAR), PLANE + RING)
    state = P(("x",) + RING, DP, None)
    rows = P(PLANE + RING, None)
    return jax.shard_map(
        per_device,
        mesh=fine,
        in_specs=(state, state, state, state, P(), P(), rows, rows, rows),
        out_specs=(state, state, state, rows),
        check_vma=False,
    )
```

```python
import jax
import jax.numpy as jnp
from jax import lax
from jax.experimental import pallas as pl
from jax.experimental.pallas import tpu as pltpu
from jax.sharding import Mesh, PartitionSpec as P

beta_one = 0.9
beta_two = 0.95
epsilon = 1e-08
learn_rate = 0.001
decay_rate = 0.1
step_count = 10

Y, CORE, X, Z = 4, 2, 4, 16
NEAR = 2
SLOTS = 6
DP = ("y", "c")
PLANE = ("y", "c", "x")
RING = ("far", "near")
SHARE = Z // (Y * CORE)
bf16, f32 = jnp.bfloat16, jnp.float32


def adamw(master, moment_one, moment_two, gradients, factor):
    scaled = gradients.astype(f32) * factor
    new_one = beta_one * moment_one + (1.0 - beta_one) * scaled
    new_two = beta_two * moment_two + (1.0 - beta_two) * scaled * scaled
    corrected_one = new_one / (1.0 - beta_one**step_count)
    corrected_two = new_two / (1.0 - beta_two**step_count)
    step_size = corrected_one / (jnp.sqrt(corrected_two) + epsilon) + decay_rate * master
    return (master - learn_rate * step_size, new_one, new_two)


def swap(array, axes):
    return lax.all_to_all(array, axes, split_axis=0, concat_axis=0, tiled=True)


def limit(mebibytes):
    return pltpu.CompilerParams(vmem_limit_bytes=mebibytes * 2**20)


def spread_squares(values, sent):
    value = values[...].astype(f32)
    sent[...] = jnp.full(sent.shape, jnp.sum(value * value), f32)


def spread_sum(values, sent):
    sent[...] = jnp.broadcast_to(jnp.sum(values[...], axis=0, keepdims=True), sent.shape)


def spread(kernel, operand, axes):
    return pl.pallas_call(
        kernel,
        out_shape=jax.ShapeDtypeStruct((lax.axis_size(axes), 1, 128), f32),
        compiler_params=limit(2),
    )(operand)


PLANE_AT, GROUP_AT, SLOT_AT, BACK, MOVED, MY_X, OVER, PICK_AT, PLAN = 0, 4, 8, 12, 13, 14, 15, 16, 32


def make_plan(old_host, new_host, plan, source, target, rank):
    my_x = lax.axis_index("x")
    my_group = lax.axis_index("far")
    my_z = my_group * NEAR + lax.axis_index("near")

    @pl.loop(0, X * Z)
    def _(expert):
        source[new_host[expert]] = old_host[expert]
        target[old_host[expert]] = new_host[expert]

    for k in range(SLOTS):
        plan[PICK_AT + k] = 0
    over = jnp.int32(0)
    for group in range(Z // NEAR):

        def visit(place, count, group=group):
            host = (place // NEAR) * Z + group * NEAR + lax.rem(place, NEAR)
            leaves = target[host] != host
            rank[host] = count

            @pl.when(leaves & (my_group == group) & (count < SLOTS))
            def _():
                plan[PICK_AT + count] = place

            return count + leaves.astype(jnp.int32)

        count = lax.fori_loop(0, X * NEAR, visit, jnp.int32(0))
        over = jnp.maximum(over, (count > SLOTS).astype(jnp.int32))
    for shift in range(X):
        host = source[lax.rem(my_x + shift, X) * Z + my_z]
        plan[PLANE_AT + shift] = lax.rem(host, Z)
        plan[GROUP_AT + shift] = lax.rem(host, Z) // NEAR
        plan[SLOT_AT + shift] = jnp.minimum(rank[host], SLOTS - 1)
    mine = source[my_x * Z + my_z]
    plan[BACK] = lax.rem(my_x + X - mine // Z, X)
    plan[MOVED] = (mine != my_x * Z + my_z).astype(jnp.int32)
    plan[MY_X] = my_x
    plan[OVER] = over


def plan_of(old_host, new_host):
    scalars = pl.BlockSpec(memory_space=pltpu.SMEM)
    return pl.pallas_call(
        make_plan,
        out_shape=jax.ShapeDtypeStruct((PLAN,), jnp.int32),
        in_specs=[scalars, scalars],
        out_specs=scalars,
        scratch_shapes=[pltpu.SMEM((X * Z,), jnp.int32)] * 3,
        compiler_params=limit(1),
    )(old_host, new_host)


def copy_picked(plan, *refs):
    half = len(refs) // 2
    for taken, kept in zip(refs[:half], refs[half:]):
        kept[...] = taken[...].reshape(kept.shape)


def pick_planes(plan, planes):
    rows, cols = planes.shape[1:]

    def take(shift):
        return pl.BlockSpec((1, rows, cols), lambda i, plan: (plan[PLANE_AT + shift], 0, 0))

    return pl.pallas_call(
        copy_picked,
        out_shape=[jax.ShapeDtypeStruct((rows, cols), bf16)] * X,
        grid_spec=pltpu.PrefetchScalarGridSpec(
            num_scalar_prefetch=1,
            grid=(1,),
            in_specs=[take(shift) for shift in range(X)],
            out_specs=[pl.BlockSpec((rows, cols), lambda i, plan: (0, 0))] * X,
        ),
        compiler_params=limit(60),
    )(plan, *[planes] * X)


def pick_pieces(plan, pieces):
    rows, cols = pieces.shape[3:]
    block = (1, NEAR, 1, rows, cols)

    def take(shift):
        return pl.BlockSpec(
            block, lambda i, plan: (plan[GROUP_AT + shift], 0, plan[SLOT_AT + shift], 0, 0)
        )

    return pl.pallas_call(
        copy_picked,
        out_shape=[jax.ShapeDtypeStruct((NEAR, rows, cols), bf16)] * X,
        grid_spec=pltpu.PrefetchScalarGridSpec(
            num_scalar_prefetch=1,
            grid=(1,),
            in_specs=[take(shift) for shift in range(X)],
            out_specs=[pl.BlockSpec((NEAR, rows, cols), lambda i, plan: (0, 0, 0))] * X,
        ),
        compiler_params=limit(60),
    )(plan, *[pieces] * X)


def compact(plan, pieces, slots):
    for k in range(SLOTS):
        slots[k] = pieces[plan[PICK_AT + k]]


def compacted(plan, pieces):
    return pl.pallas_call(
        compact,
        out_shape=jax.ShapeDtypeStruct((SLOTS,) + pieces.shape[1:], bf16),
        grid_spec=pltpu.PrefetchScalarGridSpec(
            num_scalar_prefetch=1,
            grid=(1,),
            in_specs=[pl.BlockSpec(pieces.shape, lambda i, plan: (0, 0, 0))],
            out_specs=pl.BlockSpec((SLOTS,) + pieces.shape[1:], lambda i, plan: (0, 0, 0)),
        ),
        compiler_params=limit(4),
    )(plan, pieces)


def finish(plan, here, one, two, three, own_one, own_two, new_one, new_two):
    new_one[...] = own_one[...]
    new_two[...] = own_two[...]

    @pl.when(plan[MOVED] == 1)
    def _():
        for shift, quarter in enumerate((here, one, two, three)):
            at = lax.rem(plan[MY_X] + X - shift, X) * NEAR
            for near in range(NEAR):
                piece = quarter[near].astype(f32)
                half = piece.shape[0] // 2
                rows = pl.ds(pl.multiple_of((at + near) * half, half), half)
                new_one[rows] = piece[:half]
                new_two[rows] = piece[half:]


def finished(plan, arrived, own_one, own_two):
    whole = pl.BlockSpec(memory_space=pltpu.VMEM)
    return pl.pallas_call(
        finish,
        out_shape=[jax.ShapeDtypeStruct(own_one.shape, f32)] * 2,
        in_specs=[pl.BlockSpec(memory_space=pltpu.SMEM)] + [whole] * 6,
        out_specs=[whole] * 2,
        compiler_params=limit(8),
    )(plan, *arrived, own_one, own_two)


def relocated_whole(old_host, new_host, own_one, own_two):
    rows, cols = own_one.shape
    quarter = rows // X
    hosts = jnp.arange(X * Z, dtype=jnp.int32)
    owner_hot = (new_host[None, :] == hosts[:, None]).astype(jnp.int32)
    source = jnp.sum(owner_hot * old_host[None, :], axis=1)
    my_x, my_z = lax.axis_index("x"), lax.axis_index(RING)
    plane_source = source.reshape(X, Z)[:, my_z]
    src_x, src_z = plane_source // Z, plane_source % Z
    moments = jnp.stack([own_one.astype(bf16), own_two.astype(bf16)])
    moments = swap(moments.reshape(2, X, quarter, cols).transpose(1, 0, 2, 3), "x")
    moments = lax.all_gather(moments.reshape(-1, cols), RING, axis=0, tiled=True)
    pieces = moments.reshape(Z, X, 2, quarter, cols)
    size = (1, 1, 2, quarter, cols)
    sent = [lax.dynamic_slice(pieces, (src_z[i], src_x[i], 0, 0, 0), size)[0, 0] for i in range(X)]
    arrived = swap(jnp.stack(sent), "x").transpose(1, 0, 2, 3).reshape(2, rows, cols)
    moved = plane_source[my_x] != my_x * Z + my_z
    return [
        jnp.where(moved, arrived[0].astype(f32), own_one),
        jnp.where(moved, arrived[1].astype(f32), own_two),
    ]


def expert_layer(rows, weights, outs):
    weight = weights[...].reshape(-1, weights.shape[-1])
    units = weight.shape[1] // 3
    projected = jnp.dot(rows[0], weight[:, : 2 * units], preferred_element_type=f32)
    hidden = (jax.nn.silu(projected[:, :units]) * projected[:, units:]).astype(bf16)
    produced = lax.dot_general(
        hidden, weight[:, 2 * units :], (((1,), (1,)), ((), ())), preferred_element_type=f32
    )
    outs[...] = produced.reshape(outs.shape).astype(bf16)


def experts(rows, weights, capacity):
    shares, row_count, width = rows.shape
    shards, _, shard_rows, cols = weights.shape
    return pl.pallas_call(
        expert_layer,
        out_shape=jax.ShapeDtypeStruct((row_count // capacity, shares, capacity, width), bf16),
        grid=(shares,),
        in_specs=[
            pl.BlockSpec((1, row_count, width), lambda j: (j, 0, 0)),
            pl.BlockSpec((shards, 1, shard_rows, cols), lambda j: (0, j, 0, 0)),
        ],
        out_specs=pl.BlockSpec((row_count // capacity, 1, capacity, width), lambda j: (0, j, 0, 0)),
        compiler_params=limit(30),
        cost_estimate=pl.CostEstimate(
            flops=2 * shares * row_count * width * cols,
            bytes_accessed=2 * (weights.size + 2 * rows.size),
            transcendentals=shares * row_count * cols // 3,
        ),
    )(rows, weights)


def shifted(blocks, size):
    return [
        lax.ppermute(block, "x", [(i, (i + shift) % size) for i in range(size)])
        for shift, block in enumerate(blocks, 1)
    ]


def per_device(
    master, moment_one, moment_two, gradients, old_host, new_host, tokens, routes, route_weights
):
    master, moment_one, moment_two, gradients = (
        item[0] for item in (master, moment_one, moment_two, gradients)
    )
    rows, cols = master.shape
    host_count = X * Z
    hosts = jnp.arange(host_count, dtype=jnp.int32)

    squares = swap(spread(spread_squares, gradients, PLANE), PLANE)
    squares = swap(spread(spread_sum, squares, RING), RING)
    square_sum = jnp.sum(squares[:, 0, 0])
    element_count = host_count * Y * CORE * rows * cols
    factor = jnp.minimum(1.0, jnp.sqrt(f32(element_count)) / (jnp.sqrt(square_sum) + 1e-06))

    plan = plan_of(old_host, new_host)

    tok_count, width = tokens.shape
    top = routes.shape[1]
    capacity = 3 * tok_count * top // (2 * host_count)
    place = ((old_host % Z) // SHARE * X + old_host // Z) * SHARE + old_host % SHARE
    route_place = jnp.sum(
        jnp.where(routes[:, :, None] == hosts[None, None, :], place[None, None, :], 0), axis=2
    ).T
    hits = route_place[None, :, :] == hosts[:, None, None]
    chosen = jnp.any(hits, axis=1)
    gate = jnp.sum(jnp.where(hits, route_weights.T[None, :, :], 0.0), axis=1)
    token_ids = jnp.arange(tok_count, dtype=jnp.int32)
    before = (token_ids[:, None] < token_ids[None, :]).astype(bf16)
    rank = jnp.dot(chosen.astype(bf16), before, preferred_element_type=f32)
    slot = jnp.where(chosen, rank, -1.0)
    slot_ids = jnp.arange(capacity, dtype=jnp.int32).astype(f32)
    taken = slot[:, None, :] == slot_ids[None, :, None]
    pick = taken.astype(bf16).reshape(-1, tok_count)
    outgoing = jnp.dot(pick, tokens, preferred_element_type=f32).astype(bf16)
    outgoing = outgoing.reshape(Y * CORE * X, SHARE * capacity, width)
    mix = jnp.where(taken, gate[:, None, :], 0.0).reshape(-1, tok_count)
    mix = mix.astype(bf16)
    outgoing, factor = lax.optimization_barrier((outgoing, factor))

    new_master, new_one, new_two = adamw(master, moment_one, moment_two, gradients, factor)
    new_master, new_one, new_two, rounded = lax.optimization_barrier(
        (new_master, new_one, new_two, new_master.astype(bf16))
    )
    gathered = lax.all_gather(rounded, RING, axis=0, tiled=True)
    piece = rows // (X * NEAR)
    pieces = jnp.concatenate(
        [item.astype(bf16).reshape(-1, piece, cols) for item in (new_one, new_two)], axis=1
    )
    pieces, outgoing = lax.optimization_barrier((swap(pieces, ("x", "near")), outgoing))
    received = swap(outgoing, PLANE)
    pieces = compacted(plan, pieces)
    pieces = lax.all_gather(pieces.reshape(-1, cols), RING, axis=0, tiled=True)

    held = pick_planes(plan, gathered.reshape(Z, rows, cols))
    masters = [held[0]] + shifted(held[1:], X)

    weights = swap(gathered.reshape(Y * CORE, SHARE * rows, cols), DP)
    weights, masters = lax.optimization_barrier((weights, masters))
    moved = plan[MOVED] == 1
    moved_master = lax.select_n(plan[BACK], *masters).astype(f32)
    weights = weights.reshape(Y * CORE, SHARE, rows, cols)
    inputs = received.reshape(-1, SHARE, capacity, width).transpose(1, 0, 2, 3)
    results = experts(inputs.reshape(SHARE, -1, width), weights, capacity).reshape(received.shape)
    results, late_plan = lax.optimization_barrier((results, plan))
    returned = swap(results, PLANE).reshape(-1, width)

    held = pick_pieces(late_plan, pieces.reshape(Z // NEAR, NEAR, SLOTS, 2 * piece, cols))
    arrived = [held[0]] + shifted(held[1:], X)
    returned, arrived[0] = lax.optimization_barrier((returned, arrived[0]))
    contract = (((0,), (0,)), ((), ()))
    mixed = lax.dot_general(mix, returned, contract, preferred_element_type=f32).astype(bf16)
    mixed, arrived = lax.optimization_barrier((mixed, arrived))
    moments = finished(plan, arrived, new_one, new_two)
    moments = lax.cond(
        plan[OVER] == 1,
        lambda: relocated_whole(old_host, new_host, new_one, new_two),
        lambda: list(moments),
    )
    return (
        jnp.where(moved, moved_master, new_master)[None],
        moments[0][None],
        moments[1][None],
        mixed,
    )


def solution(mesh):
    fine = Mesh(mesh.devices.reshape(Y, CORE, X, Z // NEAR, NEAR), PLANE + RING)
    state = P(("x",) + RING, DP, None)
    rows = P(PLANE + RING, None)
    return jax.shard_map(
        per_device,
        mesh=fine,
        in_specs=(state, state, state, state, P(), P(), rows, rows, rows),
        out_specs=(state, state, state, rows),
        check_vma=False,
    )
```

```python
import jax
import jax.numpy as jnp
from jax import lax
from jax.experimental import pallas as pl
from jax.experimental.pallas import tpu as pltpu
from jax.sharding import Mesh, PartitionSpec as P

beta_one = 0.9
beta_two = 0.95
epsilon = 1e-08
learn_rate = 0.001
decay_rate = 0.1
step_count = 10

Y, CORE, X, Z = 4, 2, 4, 16
NEAR = 2
SLOTS = 6
DP = ("y", "c")
PLANE = ("y", "c", "x")
RING = ("far", "near")
SHARE = Z // (Y * CORE)
bf16, f32 = jnp.bfloat16, jnp.float32


def adamw(master, moment_one, moment_two, gradients, factor):
    scaled = gradients.astype(f32) * factor
    new_one = beta_one * moment_one + (1.0 - beta_one) * scaled
    new_two = beta_two * moment_two + (1.0 - beta_two) * scaled * scaled
    corrected_one = new_one / (1.0 - beta_one**step_count)
    corrected_two = new_two / (1.0 - beta_two**step_count)
    step_size = corrected_one / (jnp.sqrt(corrected_two) + epsilon) + decay_rate * master
    return (master - learn_rate * step_size, new_one, new_two)


def swap(array, axes):
    return lax.all_to_all(array, axes, split_axis=0, concat_axis=0, tiled=True)


def limit(mebibytes):
    return pltpu.CompilerParams(vmem_limit_bytes=mebibytes * 2**20)


def spread_squares(values, sent):
    value = values[...].astype(f32)
    sent[...] = jnp.full(sent.shape, jnp.sum(value * value), f32)


def spread_sum(values, sent):
    sent[...] = jnp.broadcast_to(jnp.sum(values[...], axis=0, keepdims=True), sent.shape)


def spread(kernel, operand, axes):
    return pl.pallas_call(
        kernel,
        out_shape=jax.ShapeDtypeStruct((lax.axis_size(axes), 1, 128), f32),
        compiler_params=limit(2),
    )(operand)


PLANE_AT, GROUP_AT, SLOT_AT, BACK, MOVED, MY_X, OVER, PICK_AT, PLAN = 0, 4, 8, 12, 13, 14, 15, 16, 32


def make_plan(old_host, new_host, plan, source, target, rank):
    my_x = lax.axis_index("x")
    my_group = lax.axis_index("far")
    my_z = my_group * NEAR + lax.axis_index("near")

    @pl.loop(0, X * Z)
    def _(expert):
        source[new_host[expert]] = old_host[expert]
        target[old_host[expert]] = new_host[expert]

    for k in range(SLOTS):
        plan[PICK_AT + k] = 0
    over = jnp.int32(0)
    for group in range(Z // NEAR):

        def visit(place, count, group=group):
            host = (place // NEAR) * Z + group * NEAR + lax.rem(place, NEAR)
            leaves = target[host] != host
            rank[host] = count

            @pl.when(leaves & (my_group == group) & (count < SLOTS))
            def _():
                plan[PICK_AT + count] = place

            return count + leaves.astype(jnp.int32)

        count = lax.fori_loop(0, X * NEAR, visit, jnp.int32(0))
        over = jnp.maximum(over, (count > SLOTS).astype(jnp.int32))
    for shift in range(X):
        host = source[lax.rem(my_x + shift, X) * Z + my_z]
        plan[PLANE_AT + shift] = lax.rem(host, Z)
        plan[GROUP_AT + shift] = lax.rem(host, Z) // NEAR
        plan[SLOT_AT + shift] = jnp.minimum(rank[host], SLOTS - 1)
    mine = source[my_x * Z + my_z]
    plan[BACK] = lax.rem(my_x + X - mine // Z, X)
    plan[MOVED] = (mine != my_x * Z + my_z).astype(jnp.int32)
    plan[MY_X] = my_x
    plan[OVER] = over


def plan_of(old_host, new_host):
    scalars = pl.BlockSpec(memory_space=pltpu.SMEM)
    return pl.pallas_call(
        make_plan,
        out_shape=jax.ShapeDtypeStruct((PLAN,), jnp.int32),
        in_specs=[scalars, scalars],
        out_specs=scalars,
        scratch_shapes=[pltpu.SMEM((X * Z,), jnp.int32)] * 3,
        compiler_params=limit(1),
    )(old_host, new_host)


def copy_planes(plan, planes, *refs):
    done = refs[X]
    copies = [
        pltpu.make_async_copy(planes.at[plan[PLANE_AT + shift]], refs[shift], done.at[shift])
        for shift in range(X)
    ]
    for copy in copies:
        copy.start()
    for copy in copies:
        copy.wait()


def copy_pieces(plan, pieces, *refs):
    done = refs[X]
    copies = [
        pltpu.make_async_copy(
            pieces.at[plan[GROUP_AT + shift], :, plan[SLOT_AT + shift]], refs[shift], done.at[shift]
        )
        for shift in range(X)
    ]
    for copy in copies:
        copy.start()
    for copy in copies:
        copy.wait()


def picked(kernel, plan, source, shape):
    return pl.pallas_call(
        kernel,
        out_shape=[jax.ShapeDtypeStruct(shape, bf16)] * X,
        in_specs=[
            pl.BlockSpec(memory_space=pltpu.SMEM),
            pl.BlockSpec(memory_space=pl.ANY),
        ],
        out_specs=[pl.BlockSpec(memory_space=pl.ANY)] * X,
        scratch_shapes=[pltpu.SemaphoreType.DMA((X,))],
        compiler_params=limit(60),
    )(plan, source)


def compact(plan, pieces, slots):
    for k in range(SLOTS):
        slots[k] = pieces[plan[PICK_AT + k]]


def compacted(plan, pieces):
    return pl.pallas_call(
        compact,
        out_shape=jax.ShapeDtypeStruct((SLOTS,) + pieces.shape[1:], bf16),
        grid_spec=pltpu.PrefetchScalarGridSpec(
            num_scalar_prefetch=1,
            grid=(1,),
            in_specs=[pl.BlockSpec(pieces.shape, lambda i, plan: (0, 0, 0))],
            out_specs=pl.BlockSpec((SLOTS,) + pieces.shape[1:], lambda i, plan: (0, 0, 0)),
        ),
        compiler_params=limit(4),
    )(plan, pieces)


def finish(plan, here, one, two, three, own_one, own_two, new_one, new_two):
    new_one[...] = own_one[...]
    new_two[...] = own_two[...]

    @pl.when(plan[MOVED] == 1)
    def _():
        for shift, quarter in enumerate((here, one, two, three)):
            at = lax.rem(plan[MY_X] + X - shift, X) * NEAR
            for near in range(NEAR):
                piece = quarter[near].astype(f32)
                half = piece.shape[0] // 2
                rows = pl.ds(pl.multiple_of((at + near) * half, half), half)
                new_one[rows] = piece[:half]
                new_two[rows] = piece[half:]


def finished(plan, arrived, own_one, own_two):
    whole = pl.BlockSpec(memory_space=pltpu.VMEM)
    return pl.pallas_call(
        finish,
        out_shape=[jax.ShapeDtypeStruct(own_one.shape, f32)] * 2,
        in_specs=[pl.BlockSpec(memory_space=pltpu.SMEM)] + [whole] * 6,
        out_specs=[whole] * 2,
        compiler_params=limit(8),
    )(plan, *arrived, own_one, own_two)


def relocated_whole(old_host, new_host, own_one, own_two):
    rows, cols = own_one.shape
    quarter = rows // X
    hosts = jnp.arange(X * Z, dtype=jnp.int32)
    owner_hot = (new_host[None, :] == hosts[:, None]).astype(jnp.int32)
    source = jnp.sum(owner_hot * old_host[None, :], axis=1)
    my_x, my_z = lax.axis_index("x"), lax.axis_index(RING)
    plane_source = source.reshape(X, Z)[:, my_z]
    src_x, src_z = plane_source // Z, plane_source % Z
    moments = jnp.stack([own_one.astype(bf16), own_two.astype(bf16)])
    moments = swap(moments.reshape(2, X, quarter, cols).transpose(1, 0, 2, 3), "x")
    moments = lax.all_gather(moments.reshape(-1, cols), RING, axis=0, tiled=True)
    pieces = moments.reshape(Z, X, 2, quarter, cols)
    size = (1, 1, 2, quarter, cols)
    sent = [lax.dynamic_slice(pieces, (src_z[i], src_x[i], 0, 0, 0), size)[0, 0] for i in range(X)]
    arrived = swap(jnp.stack(sent), "x").transpose(1, 0, 2, 3).reshape(2, rows, cols)
    moved = plane_source[my_x] != my_x * Z + my_z
    return [
        jnp.where(moved, arrived[0].astype(f32), own_one),
        jnp.where(moved, arrived[1].astype(f32), own_two),
    ]


def expert_layer(rows, weights_in, weights_out, outs, hidden):
    units = weights_out.shape[-1]

    @pl.when(pl.program_id(1) == 0)
    def _():
        weight = weights_in[...].reshape(-1, 2 * units)
        projected = jnp.dot(rows[0], weight, preferred_element_type=f32)
        hidden[...] = (jax.nn.silu(projected[:, :units]) * projected[:, units:]).astype(bf16)

    @pl.when(pl.program_id(1) == 1)
    def _():
        weight = weights_out[...].reshape(-1, units)
        produced = lax.dot_general(
            hidden[...], weight, (((1,), (1,)), ((), ())), preferred_element_type=f32
        )
        outs[...] = produced.reshape(outs.shape).astype(bf16)


def experts(rows, weights, capacity):
    shares, row_count, width = rows.shape
    shards, _, shard_rows, cols = weights.shape
    units = cols // 3
    return pl.pallas_call(
        expert_layer,
        out_shape=jax.ShapeDtypeStruct((row_count // capacity, shares, capacity, width), bf16),
        grid=(shares, 2),
        in_specs=[
            pl.BlockSpec((1, row_count, width), lambda j, p: (j, 0, 0)),
            pl.BlockSpec((shards, 1, shard_rows, 2 * units), lambda j, p: (0, j, 0, 0)),
            pl.BlockSpec((shards, 1, shard_rows, units), lambda j, p: (0, j, 0, 2)),
        ],
        out_specs=pl.BlockSpec(
            (row_count // capacity, 1, capacity, width), lambda j, p: (0, j, 0, 0)
        ),
        scratch_shapes=[pltpu.VMEM((row_count, units), bf16)],
        compiler_params=limit(30),
        cost_estimate=pl.CostEstimate(
            flops=2 * shares * row_count * width * cols,
            bytes_accessed=2 * (weights.size + 2 * rows.size),
            transcendentals=shares * row_count * units,
        ),
    )(rows, weights, weights)


def shifted(blocks, size):
    return [
        lax.ppermute(block, "x", [(i, (i + shift) % size) for i in range(size)])
        for shift, block in enumerate(blocks, 1)
    ]


def per_device(
    master, moment_one, moment_two, gradients, old_host, new_host, tokens, routes, route_weights
):
    master, moment_one, moment_two, gradients = (
        item[0] for item in (master, moment_one, moment_two, gradients)
    )
    rows, cols = master.shape
    host_count = X * Z
    hosts = jnp.arange(host_count, dtype=jnp.int32)

    squares = swap(spread(spread_squares, gradients, PLANE), PLANE)
    squares = swap(spread(spread_sum, squares, RING), RING)
    square_sum = jnp.sum(squares[:, 0, 0])
    element_count = host_count * Y * CORE * rows * cols
    factor = jnp.minimum(1.0, jnp.sqrt(f32(element_count)) / (jnp.sqrt(square_sum) + 1e-06))

    plan = plan_of(old_host, new_host)

    tok_count, width = tokens.shape
    top = routes.shape[1]
    capacity = 3 * tok_count * top // (2 * host_count)
    place = ((old_host % Z) // SHARE * X + old_host // Z) * SHARE + old_host % SHARE
    route_place = jnp.sum(
        jnp.where(routes[:, :, None] == hosts[None, None, :], place[None, None, :], 0), axis=2
    ).T
    hits = route_place[None, :, :] == hosts[:, None, None]
    chosen = jnp.any(hits, axis=1)
    gate = jnp.sum(jnp.where(hits, route_weights.T[None, :, :], 0.0), axis=1)
    token_ids = jnp.arange(tok_count, dtype=jnp.int32)
    before = (token_ids[:, None] < token_ids[None, :]).astype(bf16)
    rank = jnp.dot(chosen.astype(bf16), before, preferred_element_type=f32)
    slot = jnp.where(chosen, rank, -1.0)
    slot_ids = jnp.arange(capacity, dtype=jnp.int32).astype(f32)
    taken = slot[:, None, :] == slot_ids[None, :, None]
    pick = taken.astype(bf16).reshape(-1, tok_count)
    outgoing = jnp.dot(pick, tokens, preferred_element_type=f32).astype(bf16)
    outgoing = outgoing.reshape(Y * CORE * X, SHARE * capacity, width)
    mix = jnp.where(taken, gate[:, None, :], 0.0).reshape(-1, tok_count)
    mix_high = mix.astype(bf16)
    mix_low = (mix - mix_high.astype(f32)).astype(bf16)
    mix = jnp.concatenate([mix_high, mix_low], axis=1)
    outgoing, factor = lax.optimization_barrier((outgoing, factor))

    new_master, new_one, new_two = adamw(master, moment_one, moment_two, gradients, factor)
    new_master, new_one, new_two, rounded = lax.optimization_barrier(
        (new_master, new_one, new_two, new_master.astype(bf16))
    )
    gathered = lax.all_gather(rounded, RING, axis=0, tiled=True)
    piece = rows // (X * NEAR)
    pieces = jnp.concatenate(
        [item.astype(bf16).reshape(-1, piece, cols) for item in (new_one, new_two)], axis=1
    )
    pieces, outgoing = lax.optimization_barrier((swap(pieces, ("x", "near")), outgoing))
    received = swap(outgoing, PLANE)
    pieces = compacted(plan, pieces)
    pieces = lax.all_gather(pieces.reshape(-1, cols), RING, axis=0, tiled=True)

    held = picked(copy_planes, plan, gathered.reshape(Z, rows, cols), (rows, cols))
    masters = [held[0]] + shifted(held[1:], X)

    weights = swap(gathered.reshape(Y * CORE, SHARE * rows, cols), DP)
    weights, masters = lax.optimization_barrier((weights, masters))
    moved = plan[MOVED] == 1
    moved_master = lax.select_n(plan[BACK], *masters).astype(f32)
    weights = weights.reshape(Y * CORE, SHARE, rows, cols)
    inputs = received.reshape(-1, SHARE, capacity, width).transpose(1, 0, 2, 3)
    results = experts(inputs.reshape(SHARE, -1, width), weights, capacity).reshape(received.shape)
    results, late_plan = lax.optimization_barrier((results, plan))
    returned = swap(results, PLANE).reshape(-1, width)

    pieces = pieces.reshape(Z // NEAR, NEAR, SLOTS, 2 * piece, cols)
    held = picked(copy_pieces, late_plan, pieces, (NEAR, 2 * piece, cols))
    arrived = [held[0]] + shifted(held[1:], X)
    returned, arrived[0] = lax.optimization_barrier((returned, arrived[0]))
    contract = (((0,), (0,)), ((), ()))
    mixed = lax.dot_general(mix, returned, contract, preferred_element_type=f32)
    mixed = (mixed[:tok_count] + mixed[tok_count:]).astype(bf16)
    mixed, arrived = lax.optimization_barrier((mixed, arrived))
    moments = finished(plan, arrived, new_one, new_two)
    moments = lax.cond(
        plan[OVER] == 1,
        lambda: relocated_whole(old_host, new_host, new_one, new_two),
        lambda: list(moments),
    )
    return (
        jnp.where(moved, moved_master, new_master)[None],
        moments[0][None],
        moments[1][None],
        mixed,
    )


def solution(mesh):
    fine = Mesh(mesh.devices.reshape(Y, CORE, X, Z // NEAR, NEAR), PLANE + RING)
    state = P(("x",) + RING, DP, None)
    rows = P(PLANE + RING, None)
    return jax.shard_map(
        per_device,
        mesh=fine,
        in_specs=(state, state, state, state, P(), P(), rows, rows, rows),
        out_specs=(state, state, state, rows),
        check_vma=False,
    )
```

```python
import jax
import jax.numpy as jnp
from jax import lax
from jax.experimental import pallas as pl
from jax.experimental.pallas import tpu as pltpu
from jax.sharding import Mesh, PartitionSpec as P

beta_one = 0.9
beta_two = 0.95
epsilon = 1e-08
learn_rate = 0.001
decay_rate = 0.1
step_count = 10

Y, CORE, X, Z = 4, 2, 4, 16
NEAR = 2
SLOTS = 6
SHIFTS = (0, 2, 1, 3)
DP = ("y", "c")
PLANE = ("y", "c", "x")
RING = ("far", "near")
SHARE = Z // (Y * CORE)
bf16, f32 = jnp.bfloat16, jnp.float32


def adamw(master, moment_one, moment_two, gradients, factor):
    scaled = gradients.astype(f32) * factor
    new_one = beta_one * moment_one + (1.0 - beta_one) * scaled
    new_two = beta_two * moment_two + (1.0 - beta_two) * scaled * scaled
    corrected_one = new_one / (1.0 - beta_one**step_count)
    corrected_two = new_two / (1.0 - beta_two**step_count)
    step_size = corrected_one / (jnp.sqrt(corrected_two) + epsilon) + decay_rate * master
    return (master - learn_rate * step_size, new_one, new_two)


def swap(array, axes):
    return lax.all_to_all(array, axes, split_axis=0, concat_axis=0, tiled=True)


def limit(mebibytes):
    return pltpu.CompilerParams(vmem_limit_bytes=mebibytes * 2**20)


def spread_squares(values, sent):
    value = values[...].astype(f32)
    sent[...] = jnp.full(sent.shape, jnp.sum(value * value), f32)


def spread_sum(values, sent):
    sent[...] = jnp.broadcast_to(jnp.sum(values[...], axis=0, keepdims=True), sent.shape)


def spread(kernel, operand, axes):
    return pl.pallas_call(
        kernel,
        out_shape=jax.ShapeDtypeStruct((lax.axis_size(axes), 1, 128), f32),
        compiler_params=limit(2),
    )(operand)


PLANE_AT, GROUP_AT, SLOT_AT, BACK, MOVED, MY_X, OVER, PICK_AT, PLAN = 0, 4, 8, 12, 13, 14, 15, 16, 32


def make_plan(old_host, new_host, plan, source, target, rank):
    my_x = lax.axis_index("x")
    my_group = lax.axis_index("far")
    my_z = my_group * NEAR + lax.axis_index("near")

    @pl.loop(0, X * Z)
    def _(expert):
        source[new_host[expert]] = old_host[expert]
        target[old_host[expert]] = new_host[expert]

    for k in range(SLOTS):
        plan[PICK_AT + k] = 0
    over = jnp.int32(0)
    for group in range(Z // NEAR):

        def visit(place, count, group=group):
            host = (place // NEAR) * Z + group * NEAR + lax.rem(place, NEAR)
            leaves = target[host] != host
            rank[host] = count

            @pl.when(leaves & (my_group == group) & (count < SLOTS))
            def _():
                plan[PICK_AT + count] = place

            return count + leaves.astype(jnp.int32)

        count = lax.fori_loop(0, X * NEAR, visit, jnp.int32(0))
        over = jnp.maximum(over, (count > SLOTS).astype(jnp.int32))
    for shift in range(X):
        host = source[lax.rem(my_x + shift, X) * Z + my_z]
        plan[PLANE_AT + shift] = lax.rem(host, Z)
        plan[GROUP_AT + shift] = lax.rem(host, Z) // NEAR
        plan[SLOT_AT + shift] = jnp.minimum(rank[host], SLOTS - 1)
    mine = source[my_x * Z + my_z]
    plan[BACK] = lax.rem(my_x + X - mine // Z, X)
    plan[MOVED] = (mine != my_x * Z + my_z).astype(jnp.int32)
    plan[MY_X] = my_x
    plan[OVER] = over


def plan_of(old_host, new_host):
    scalars = pl.BlockSpec(memory_space=pltpu.SMEM)
    return pl.pallas_call(
        make_plan,
        out_shape=jax.ShapeDtypeStruct((PLAN,), jnp.int32),
        in_specs=[scalars, scalars],
        out_specs=scalars,
        scratch_shapes=[pltpu.SMEM((X * Z,), jnp.int32)] * 3,
        compiler_params=limit(1),
    )(old_host, new_host)


def copy_planes(plan, planes, *refs):
    done = refs[X]
    copies = [
        pltpu.make_async_copy(planes.at[plan[PLANE_AT + shift]], refs[i], done.at[i])
        for i, shift in enumerate(SHIFTS)
    ]
    for copy in copies:
        copy.start()
    for copy in copies:
        copy.wait()


def copy_pieces(plan, pieces, *refs):
    done = refs[X]
    copies = [
        pltpu.make_async_copy(
            pieces.at[plan[GROUP_AT + shift], :, plan[SLOT_AT + shift]], refs[i], done.at[i]
        )
        for i, shift in enumerate(SHIFTS)
    ]
    for copy in copies:
        copy.start()
    for copy in copies:
        copy.wait()


def picked(kernel, plan, source, shape):
    return pl.pallas_call(
        kernel,
        out_shape=[jax.ShapeDtypeStruct(shape, bf16)] * X,
        in_specs=[
            pl.BlockSpec(memory_space=pltpu.SMEM),
            pl.BlockSpec(memory_space=pl.ANY),
        ],
        out_specs=[pl.BlockSpec(memory_space=pltpu.VMEM)] * X,
        scratch_shapes=[pltpu.SemaphoreType.DMA((X,))],
        compiler_params=limit(60),
    )(plan, source)


def compact(plan, pieces, slots):
    for k in range(SLOTS):
        slots[k] = pieces[plan[PICK_AT + k]]


def compacted(plan, pieces):
    return pl.pallas_call(
        compact,
        out_shape=jax.ShapeDtypeStruct((SLOTS,) + pieces.shape[1:], bf16),
        grid_spec=pltpu.PrefetchScalarGridSpec(
            num_scalar_prefetch=1,
            grid=(1,),
            in_specs=[pl.BlockSpec(pieces.shape, lambda i, plan: (0, 0, 0))],
            out_specs=pl.BlockSpec((SLOTS,) + pieces.shape[1:], lambda i, plan: (0, 0, 0)),
        ),
        compiler_params=limit(4),
    )(plan, pieces)


def finish(plan, here, one, two, three, own_one, own_two, new_one, new_two):
    new_one[...] = own_one[...]
    new_two[...] = own_two[...]

    @pl.when(plan[MOVED] == 1)
    def _():
        for shift, quarter in zip(SHIFTS, (here, one, two, three)):
            at = lax.rem(plan[MY_X] + X - shift, X) * NEAR
            for near in range(NEAR):
                piece = quarter[near].astype(f32)
                half = piece.shape[0] // 2
                rows = pl.ds(pl.multiple_of((at + near) * half, half), half)
                new_one[rows] = piece[:half]
                new_two[rows] = piece[half:]


def finished(plan, arrived, own_one, own_two):
    whole = pl.BlockSpec(memory_space=pltpu.VMEM)
    return pl.pallas_call(
        finish,
        out_shape=[jax.ShapeDtypeStruct(own_one.shape, f32)] * 2,
        in_specs=[pl.BlockSpec(memory_space=pltpu.SMEM)] + [whole] * 6,
        out_specs=[whole] * 2,
        compiler_params=limit(8),
    )(plan, *arrived, own_one, own_two)


def relocated_whole(old_host, new_host, own_one, own_two):
    rows, cols = own_one.shape
    quarter = rows // X
    hosts = jnp.arange(X * Z, dtype=jnp.int32)
    owner_hot = (new_host[None, :] == hosts[:, None]).astype(jnp.int32)
    source = jnp.sum(owner_hot * old_host[None, :], axis=1)
    my_x, my_z = lax.axis_index("x"), lax.axis_index(RING)
    plane_source = source.reshape(X, Z)[:, my_z]
    src_x, src_z = plane_source // Z, plane_source % Z
    moments = jnp.stack([own_one.astype(bf16), own_two.astype(bf16)])
    moments = swap(moments.reshape(2, X, quarter, cols).transpose(1, 0, 2, 3), "x")
    moments = lax.all_gather(moments.reshape(-1, cols), RING, axis=0, tiled=True)
    pieces = moments.reshape(Z, X, 2, quarter, cols)
    size = (1, 1, 2, quarter, cols)
    sent = [lax.dynamic_slice(pieces, (src_z[i], src_x[i], 0, 0, 0), size)[0, 0] for i in range(X)]
    arrived = swap(jnp.stack(sent), "x").transpose(1, 0, 2, 3).reshape(2, rows, cols)
    moved = plane_source[my_x] != my_x * Z + my_z
    return [
        jnp.where(moved, arrived[0].astype(f32), own_one),
        jnp.where(moved, arrived[1].astype(f32), own_two),
    ]


def expert_layer(rows, weights_in, weights_out, outs, hidden):
    units = weights_out.shape[-1]

    @pl.when(pl.program_id(1) == 0)
    def _():
        weight = weights_in[...].reshape(-1, 2 * units)
        projected = jnp.dot(rows[0], weight, preferred_element_type=f32)
        hidden[...] = (jax.nn.silu(projected[:, :units]) * projected[:, units:]).astype(bf16)

    @pl.when(pl.program_id(1) == 1)
    def _():
        weight = weights_out[...].reshape(-1, units)
        produced = lax.dot_general(
            hidden[...], weight, (((1,), (1,)), ((), ())), preferred_element_type=f32
        )
        outs[...] = produced.reshape(outs.shape).astype(bf16)


def experts(rows, weights, capacity):
    shares, row_count, width = rows.shape
    shards, _, shard_rows, cols = weights.shape
    units = cols // 3
    return pl.pallas_call(
        expert_layer,
        out_shape=jax.ShapeDtypeStruct((row_count // capacity, shares, capacity, width), bf16),
        grid=(shares, 2),
        in_specs=[
            pl.BlockSpec((1, row_count, width), lambda j, p: (j, 0, 0)),
            pl.BlockSpec((shards, 1, shard_rows, 2 * units), lambda j, p: (0, j, 0, 0)),
            pl.BlockSpec((shards, 1, shard_rows, units), lambda j, p: (0, j, 0, 2)),
        ],
        out_specs=pl.BlockSpec(
            (row_count // capacity, 1, capacity, width), lambda j, p: (0, j, 0, 0)
        ),
        scratch_shapes=[pltpu.VMEM((row_count, units), bf16)],
        compiler_params=limit(30),
        cost_estimate=pl.CostEstimate(
            flops=2 * shares * row_count * width * cols,
            bytes_accessed=2 * (weights.size + 2 * rows.size),
            transcendentals=shares * row_count * units,
        ),
    )(rows, weights, weights)


def shifted(blocks):
    arrived = blocks[:1]
    for block, shift in zip(blocks[1:], SHIFTS[1:]):
        arrived.append(lax.ppermute(block, "x", [(i, (i + shift) % X) for i in range(X)]))
    return arrived


def per_device(
    master, moment_one, moment_two, gradients, old_host, new_host, tokens, routes, route_weights
):
    master, moment_one, moment_two, gradients = (
        item[0] for item in (master, moment_one, moment_two, gradients)
    )
    rows, cols = master.shape
    host_count = X * Z
    hosts = jnp.arange(host_count, dtype=jnp.int32)

    squares = swap(spread(spread_squares, gradients, PLANE), PLANE)
    squares = swap(spread(spread_sum, squares, RING), RING)
    square_sum = jnp.sum(squares[:, 0, 0])
    element_count = host_count * Y * CORE * rows * cols
    factor = jnp.minimum(1.0, jnp.sqrt(f32(element_count)) / (jnp.sqrt(square_sum) + 1e-06))

    plan = plan_of(old_host, new_host)

    tok_count, width = tokens.shape
    top = routes.shape[1]
    capacity = 3 * tok_count * top // (2 * host_count)
    place = ((old_host % Z) // SHARE * X + old_host // Z) * SHARE + old_host % SHARE
    route_place = jnp.sum(
        jnp.where(routes[:, :, None] == hosts[None, None, :], place[None, None, :], 0), axis=2
    ).T
    hits = route_place[None, :, :] == hosts[:, None, None]
    chosen = jnp.any(hits, axis=1)
    gate = jnp.sum(jnp.where(hits, route_weights.T[None, :, :], 0.0), axis=1)
    token_ids = jnp.arange(tok_count, dtype=jnp.int32)
    before = (token_ids[:, None] < token_ids[None, :]).astype(bf16)
    rank = jnp.dot(chosen.astype(bf16), before, preferred_element_type=f32)
    slot = jnp.where(chosen, rank, -1.0)
    slot_ids = jnp.arange(capacity, dtype=jnp.int32).astype(f32)
    taken = slot[:, None, :] == slot_ids[None, :, None]
    pick = taken.astype(bf16).reshape(-1, tok_count)
    outgoing = jnp.dot(pick, tokens, preferred_element_type=f32).astype(bf16)
    outgoing = outgoing.reshape(Y * CORE * X, SHARE * capacity, width)
    mix = jnp.where(taken, gate[:, None, :], 0.0).reshape(-1, tok_count)
    mix_high = mix.astype(bf16)
    mix_low = (mix - mix_high.astype(f32)).astype(bf16)
    mix = jnp.concatenate([mix_high, mix_low], axis=1)
    outgoing, factor = lax.optimization_barrier((outgoing, factor))

    new_master, new_one, new_two = adamw(master, moment_one, moment_two, gradients, factor)
    new_master, new_one, new_two, rounded = lax.optimization_barrier(
        (new_master, new_one, new_two, new_master.astype(bf16))
    )
    gathered = lax.all_gather(rounded, RING, axis=0, tiled=True)
    piece = rows // (X * NEAR)
    pieces = jnp.concatenate(
        [item.astype(bf16).reshape(-1, piece, cols) for item in (new_one, new_two)], axis=1
    )
    pieces, outgoing = lax.optimization_barrier((swap(pieces, ("x", "near")), outgoing))
    received = swap(outgoing, PLANE)
    pieces = compacted(plan, pieces)
    pieces = lax.all_gather(pieces.reshape(-1, cols), RING, axis=0, tiled=True)

    held = picked(copy_planes, plan, gathered.reshape(Z, rows, cols), (rows, cols))
    masters = shifted(list(held))

    weights = swap(gathered.reshape(Y * CORE, SHARE * rows, cols), DP)
    weights, masters = lax.optimization_barrier((weights, masters))
    moved = plan[MOVED] == 1
    moved_master = lax.select_n(plan[BACK], *[masters[SHIFTS.index(shift)] for shift in range(X)]).astype(f32)
    weights = weights.reshape(Y * CORE, SHARE, rows, cols)
    inputs = received.reshape(-1, SHARE, capacity, width).transpose(1, 0, 2, 3)
    results = experts(inputs.reshape(SHARE, -1, width), weights, capacity).reshape(received.shape)
    results, late_plan = lax.optimization_barrier((results, plan))
    returned = swap(results, PLANE).reshape(-1, width)

    pieces = pieces.reshape(Z // NEAR, NEAR, SLOTS, 2 * piece, cols)
    held = picked(copy_pieces, late_plan, pieces, (NEAR, 2 * piece, cols))
    arrived = shifted(list(held))
    returned, arrived[0] = lax.optimization_barrier((returned, arrived[0]))
    contract = (((0,), (0,)), ((), ()))
    mixed = lax.dot_general(mix, returned, contract, preferred_element_type=f32)
    mixed = (mixed[:tok_count] + mixed[tok_count:]).astype(bf16)
    mixed, arrived = lax.optimization_barrier((mixed, arrived))
    moments = finished(plan, arrived, new_one, new_two)
    moments = lax.cond(
        plan[OVER] == 1,
        lambda: relocated_whole(old_host, new_host, new_one, new_two),
        lambda: list(moments),
    )
    return (
        jnp.where(moved, moved_master, new_master)[None],
        moments[0][None],
        moments[1][None],
        mixed,
    )


def solution(mesh):
    fine = Mesh(mesh.devices.reshape(Y, CORE, X, Z // NEAR, NEAR), PLANE + RING)
    state = P(("x",) + RING, DP, None)
    rows = P(PLANE + RING, None)
    return jax.shard_map(
        per_device,
        mesh=fine,
        in_specs=(state, state, state, state, P(), P(), rows, rows, rows),
        out_specs=(state, state, state, rows),
        check_vma=False,
    )
```

```python
import jax
import jax.numpy as jnp
from jax import lax
from jax.experimental import pallas as pl
from jax.experimental.pallas import tpu as pltpu
from jax.sharding import Mesh, PartitionSpec as P

beta_one = 0.9
beta_two = 0.95
epsilon = 1e-08
learn_rate = 0.001
decay_rate = 0.1
step_count = 10

Y, CORE, X, Z = 4, 2, 4, 16
NEAR = 2
SLOTS = 6
SHIFTS = (0, 2, 1, 3)
DP = ("y", "c")
PLANE = ("y", "c", "x")
RING = ("far", "near")
SHARE = Z // (Y * CORE)
bf16, f32 = jnp.bfloat16, jnp.float32


def adamw(master, moment_one, moment_two, gradients, factor):
    scaled = gradients.astype(f32) * factor
    new_one = beta_one * moment_one + (1.0 - beta_one) * scaled
    new_two = beta_two * moment_two + (1.0 - beta_two) * scaled * scaled
    corrected_one = new_one / (1.0 - beta_one**step_count)
    corrected_two = new_two / (1.0 - beta_two**step_count)
    step_size = corrected_one / (jnp.sqrt(corrected_two) + epsilon) + decay_rate * master
    return (master - learn_rate * step_size, new_one, new_two)


def swap(array, axes):
    return lax.all_to_all(array, axes, split_axis=0, concat_axis=0, tiled=True)


def limit(mebibytes):
    return pltpu.CompilerParams(vmem_limit_bytes=mebibytes * 2**20)


def spread_squares(values, sent):
    value = values[...].astype(f32)
    sent[...] = jnp.full(sent.shape, jnp.sum(value * value), f32)


def spread_sum(values, sent):
    sent[...] = jnp.broadcast_to(jnp.sum(values[...], axis=0, keepdims=True), sent.shape)


def spread(kernel, operand, axes):
    return pl.pallas_call(
        kernel,
        out_shape=jax.ShapeDtypeStruct((lax.axis_size(axes), 1, 128), f32),
        compiler_params=limit(2),
    )(operand)


PLANE_AT, GROUP_AT, SLOT_AT, BACK, MOVED, MY_X, OVER, PICK_AT, PLAN = 0, 4, 8, 12, 13, 14, 15, 16, 32


def make_plan(old_host, new_host, plan, source, target, rank):
    my_x = lax.axis_index("x")
    my_group = lax.axis_index("far")
    my_z = my_group * NEAR + lax.axis_index("near")

    @pl.loop(0, X * Z)
    def _(expert):
        source[new_host[expert]] = old_host[expert]
        target[old_host[expert]] = new_host[expert]

    for k in range(SLOTS):
        plan[PICK_AT + k] = 0
    over = jnp.int32(0)
    for group in range(Z // NEAR):

        def visit(place, count, group=group):
            host = (place // NEAR) * Z + group * NEAR + lax.rem(place, NEAR)
            leaves = target[host] != host
            rank[host] = count

            @pl.when(leaves & (my_group == group) & (count < SLOTS))
            def _():
                plan[PICK_AT + count] = place

            return count + leaves.astype(jnp.int32)

        count = lax.fori_loop(0, X * NEAR, visit, jnp.int32(0))
        over = jnp.maximum(over, (count > SLOTS).astype(jnp.int32))
    for shift in range(X):
        host = source[lax.rem(my_x + shift, X) * Z + my_z]
        plan[PLANE_AT + shift] = lax.rem(host, Z)
        plan[GROUP_AT + shift] = lax.rem(host, Z) // NEAR
        plan[SLOT_AT + shift] = jnp.minimum(rank[host], SLOTS - 1)
    mine = source[my_x * Z + my_z]
    plan[BACK] = lax.rem(my_x + X - mine // Z, X)
    plan[MOVED] = (mine != my_x * Z + my_z).astype(jnp.int32)
    plan[MY_X] = my_x
    plan[OVER] = over


def plan_of(old_host, new_host):
    scalars = pl.BlockSpec(memory_space=pltpu.SMEM)
    return pl.pallas_call(
        make_plan,
        out_shape=jax.ShapeDtypeStruct((PLAN,), jnp.int32),
        in_specs=[scalars, scalars],
        out_specs=scalars,
        scratch_shapes=[pltpu.SMEM((X * Z,), jnp.int32)] * 3,
        compiler_params=limit(1),
    )(old_host, new_host)


def copy_planes(plan, planes, *refs):
    done = refs[X]
    copies = [
        pltpu.make_async_copy(planes.at[plan[PLANE_AT + shift]], refs[i], done.at[i])
        for i, shift in enumerate(SHIFTS)
    ]
    for copy in copies:
        copy.start()
    for copy in copies:
        copy.wait()


def copy_pieces(plan, pieces, *refs):
    done = refs[X]
    copies = [
        pltpu.make_async_copy(
            pieces.at[plan[GROUP_AT + shift], :, plan[SLOT_AT + shift]], refs[i], done.at[i]
        )
        for i, shift in enumerate(SHIFTS)
    ]
    for copy in copies:
        copy.start()
    for copy in copies:
        copy.wait()


def picked(kernel, plan, source, shape):
    return pl.pallas_call(
        kernel,
        out_shape=[jax.ShapeDtypeStruct(shape, bf16)] * X,
        in_specs=[
            pl.BlockSpec(memory_space=pltpu.SMEM),
            pl.BlockSpec(memory_space=pl.ANY),
        ],
        out_specs=[pl.BlockSpec(memory_space=pltpu.VMEM)] * X,
        scratch_shapes=[pltpu.SemaphoreType.DMA((X,))],
        compiler_params=limit(60),
    )(plan, source)


def compact(plan, pieces, slots):
    for k in range(SLOTS):
        slots[k] = pieces[plan[PICK_AT + k]]


def compacted(plan, pieces):
    return pl.pallas_call(
        compact,
        out_shape=jax.ShapeDtypeStruct((SLOTS,) + pieces.shape[1:], bf16),
        grid_spec=pltpu.PrefetchScalarGridSpec(
            num_scalar_prefetch=1,
            grid=(1,),
            in_specs=[pl.BlockSpec(pieces.shape, lambda i, plan: (0, 0, 0))],
            out_specs=pl.BlockSpec((SLOTS,) + pieces.shape[1:], lambda i, plan: (0, 0, 0)),
        ),
        compiler_params=limit(4),
    )(plan, pieces)


def finish(plan, here, one, two, three, own_one, own_two, new_one, new_two):
    new_one[...] = own_one[...]
    new_two[...] = own_two[...]

    @pl.when(plan[MOVED] == 1)
    def _():
        for shift, quarter in zip(SHIFTS, (here, one, two, three)):
            at = lax.rem(plan[MY_X] + X - shift, X) * NEAR
            for near in range(NEAR):
                piece = quarter[near].astype(f32)
                half = piece.shape[0] // 2
                rows = pl.ds(pl.multiple_of((at + near) * half, half), half)
                new_one[rows] = piece[:half]
                new_two[rows] = piece[half:]


def finished(plan, arrived, own_one, own_two):
    whole = pl.BlockSpec(memory_space=pltpu.VMEM)
    return pl.pallas_call(
        finish,
        out_shape=[jax.ShapeDtypeStruct(own_one.shape, f32)] * 2,
        in_specs=[pl.BlockSpec(memory_space=pltpu.SMEM)] + [whole] * 6,
        out_specs=[whole] * 2,
        compiler_params=limit(8),
    )(plan, *arrived, own_one, own_two)


def relocated_whole(old_host, new_host, own_one, own_two):
    rows, cols = own_one.shape
    quarter = rows // X
    hosts = jnp.arange(X * Z, dtype=jnp.int32)
    owner_hot = (new_host[None, :] == hosts[:, None]).astype(jnp.int32)
    source = jnp.sum(owner_hot * old_host[None, :], axis=1)
    my_x, my_z = lax.axis_index("x"), lax.axis_index(RING)
    plane_source = source.reshape(X, Z)[:, my_z]
    src_x, src_z = plane_source // Z, plane_source % Z
    moments = jnp.stack([own_one.astype(bf16), own_two.astype(bf16)])
    moments = swap(moments.reshape(2, X, quarter, cols).transpose(1, 0, 2, 3), "x")
    moments = lax.all_gather(moments.reshape(-1, cols), RING, axis=0, tiled=True)
    pieces = moments.reshape(Z, X, 2, quarter, cols)
    size = (1, 1, 2, quarter, cols)
    sent = [lax.dynamic_slice(pieces, (src_z[i], src_x[i], 0, 0, 0), size)[0, 0] for i in range(X)]
    arrived = swap(jnp.stack(sent), "x").transpose(1, 0, 2, 3).reshape(2, rows, cols)
    moved = plane_source[my_x] != my_x * Z + my_z
    return [
        jnp.where(moved, arrived[0].astype(f32), own_one),
        jnp.where(moved, arrived[1].astype(f32), own_two),
    ]


def expert_layer(rows, weights_in, weights_out, outs, hidden):
    units = weights_out.shape[-1]

    @pl.when(pl.program_id(1) == 0)
    def _():
        weight = weights_in[...].reshape(-1, 2 * units)
        projected = jnp.dot(rows[0], weight, preferred_element_type=f32)
        hidden[...] = (jax.nn.silu(projected[:, :units]) * projected[:, units:]).astype(bf16)

    half = hidden.shape[0] // 2
    for i in range(2):

        @pl.when(pl.program_id(1) == i + 1)
        def _(i=i):
            weight = weights_out[...].reshape(-1, units)
            rows_in = hidden[i * half : (i + 1) * half]
            produced = lax.dot_general(
                rows_in, weight, (((1,), (1,)), ((), ())), preferred_element_type=f32
            )
            outs[...] = produced.reshape(outs.shape).astype(bf16)


def experts(rows, weights, capacity):
    shares, row_count, width = rows.shape
    shards, _, shard_rows, cols = weights.shape
    units = cols // 3
    return pl.pallas_call(
        expert_layer,
        out_shape=jax.ShapeDtypeStruct((row_count // capacity, shares, capacity, width), bf16),
        grid=(shares, 3),
        in_specs=[
            pl.BlockSpec((1, row_count, width), lambda j, p: (j, 0, 0)),
            pl.BlockSpec((shards, 1, shard_rows, 2 * units), lambda j, p: (0, j, 0, 0)),
            pl.BlockSpec((shards, 1, shard_rows, units), lambda j, p: (0, j, 0, 2)),
        ],
        out_specs=pl.BlockSpec(
            (row_count // capacity // 2, 1, capacity, width), lambda j, p: (p // 2, j, 0, 0)
        ),
        scratch_shapes=[pltpu.VMEM((row_count, units), bf16)],
        compiler_params=limit(30),
        cost_estimate=pl.CostEstimate(
            flops=2 * shares * row_count * width * cols,
            bytes_accessed=2 * (weights.size + 2 * rows.size),
            transcendentals=shares * row_count * units,
        ),
    )(rows, weights, weights)


def shifted(blocks):
    arrived = blocks[:1]
    for block, shift in zip(blocks[1:], SHIFTS[1:]):
        arrived.append(lax.ppermute(block, "x", [(i, (i + shift) % X) for i in range(X)]))
    return arrived


def per_device(
    master, moment_one, moment_two, gradients, old_host, new_host, tokens, routes, route_weights
):
    master, moment_one, moment_two, gradients = (
        item[0] for item in (master, moment_one, moment_two, gradients)
    )
    rows, cols = master.shape
    host_count = X * Z
    hosts = jnp.arange(host_count, dtype=jnp.int32)

    squares = swap(spread(spread_squares, gradients, PLANE), PLANE)
    squares = swap(spread(spread_sum, squares, RING), RING)
    square_sum = jnp.sum(squares[:, 0, 0])
    element_count = host_count * Y * CORE * rows * cols
    factor = jnp.minimum(1.0, jnp.sqrt(f32(element_count)) / (jnp.sqrt(square_sum) + 1e-06))

    plan = plan_of(old_host, new_host)

    tok_count, width = tokens.shape
    top = routes.shape[1]
    capacity = 3 * tok_count * top // (2 * host_count)
    place = ((old_host % Z) // SHARE * X + old_host // Z) * SHARE + old_host % SHARE
    route_place = jnp.sum(
        jnp.where(routes[:, :, None] == hosts[None, None, :], place[None, None, :], 0), axis=2
    ).T
    hits = route_place[None, :, :] == hosts[:, None, None]
    chosen = jnp.any(hits, axis=1)
    gate = jnp.sum(jnp.where(hits, route_weights.T[None, :, :], 0.0), axis=1)
    token_ids = jnp.arange(tok_count, dtype=jnp.int32)
    before = (token_ids[:, None] < token_ids[None, :]).astype(bf16)
    rank = jnp.dot(chosen.astype(bf16), before, preferred_element_type=f32)
    slot = jnp.where(chosen, rank, -1.0)
    slot_ids = jnp.arange(capacity, dtype=jnp.int32).astype(f32)
    taken = slot[:, None, :] == slot_ids[None, :, None]
    pick = taken.astype(bf16).reshape(-1, tok_count)
    outgoing = jnp.dot(pick, tokens, preferred_element_type=f32).astype(bf16)
    outgoing = outgoing.reshape(Y * CORE * X, SHARE * capacity, width)
    mix = jnp.where(taken, gate[:, None, :], 0.0).reshape(-1, tok_count)
    mix_high = mix.astype(bf16)
    mix_low = (mix - mix_high.astype(f32)).astype(bf16)
    mix = jnp.concatenate([mix_high, mix_low], axis=1)
    outgoing, factor = lax.optimization_barrier((outgoing, factor))

    new_master, new_one, new_two = adamw(master, moment_one, moment_two, gradients, factor)
    new_master, new_one, new_two, rounded = lax.optimization_barrier(
        (new_master, new_one, new_two, new_master.astype(bf16))
    )
    gathered = lax.all_gather(rounded, RING, axis=0, tiled=True)
    piece = rows // (X * NEAR)
    pieces = jnp.concatenate(
        [item.astype(bf16).reshape(-1, piece, cols) for item in (new_one, new_two)], axis=1
    )
    pieces, outgoing = lax.optimization_barrier((swap(pieces, ("x", "near")), outgoing))
    received = swap(outgoing, PLANE)
    pieces = compacted(plan, pieces)
    pieces = lax.all_gather(pieces.reshape(-1, cols), RING, axis=0, tiled=True)

    held = picked(copy_planes, plan, gathered.reshape(Z, rows, cols), (rows, cols))
    masters = shifted(list(held))

    weights = swap(gathered.reshape(Y * CORE, SHARE * rows, cols), DP)
    weights, masters = lax.optimization_barrier((weights, masters))
    moved = plan[MOVED] == 1
    moved_master = lax.select_n(plan[BACK], *[masters[SHIFTS.index(shift)] for shift in range(X)]).astype(f32)
    weights = weights.reshape(Y * CORE, SHARE, rows, cols)
    inputs = received.reshape(-1, SHARE, capacity, width).transpose(1, 0, 2, 3)
    results = experts(inputs.reshape(SHARE, -1, width), weights, capacity).reshape(received.shape)
    results, late_plan = lax.optimization_barrier((results, plan))
    returned = swap(results, PLANE).reshape(-1, width)

    pieces = pieces.reshape(Z // NEAR, NEAR, SLOTS, 2 * piece, cols)
    held = picked(copy_pieces, late_plan, pieces, (NEAR, 2 * piece, cols))
    arrived = shifted(list(held))
    returned, arrived[0] = lax.optimization_barrier((returned, arrived[0]))
    contract = (((0,), (0,)), ((), ()))
    mixed = lax.dot_general(mix, returned, contract, preferred_element_type=f32)
    mixed = (mixed[:tok_count] + mixed[tok_count:]).astype(bf16)
    mixed, arrived = lax.optimization_barrier((mixed, arrived))
    moments = finished(plan, arrived, new_one, new_two)
    moments = lax.cond(
        plan[OVER] == 1,
        lambda: relocated_whole(old_host, new_host, new_one, new_two),
        lambda: list(moments),
    )
    return (
        jnp.where(moved, moved_master, new_master)[None],
        moments[0][None],
        moments[1][None],
        mixed,
    )


def solution(mesh):
    fine = Mesh(mesh.devices.reshape(Y, CORE, X, Z // NEAR, NEAR), PLANE + RING)
    state = P(("x",) + RING, DP, None)
    rows = P(PLANE + RING, None)
    return jax.shard_map(
        per_device,
        mesh=fine,
        in_specs=(state, state, state, state, P(), P(), rows, rows, rows),
        out_specs=(state, state, state, rows),
        check_vma=False,
    )
```
